512 devices in a mesh: wave: 64 (over z, x), lev: 8 (over y, core).
Axes of the slice: x: 4, y: 4, z: 16, core: 2. Of those that a mesh axis runs over, the one named last changes fastest.
Arguments:
- spectra: bfloat16 [8, 1280, 8, 1280], P('lev', 'wave'), may hold values from -0.0048828125 to 0.0048828125
- wave_order: int32 [1280], replicated, may hold values from 0 to 1279, as said below
- truncation: int32 [1280], replicated, may hold values from 160 to 1280, as said below
Outputs:
- flux_spectra: float32 [8, 1280, 8, 1280], P('lev', 'wave')
The draws below stay inside these ranges and needn't reach their ends.
Inputs may be any that keep to these rules, and one draw needn't show every extreme that they name: `wave_order`: A permutation of 0 to 1279; in each block of 20 rows the r-th row holds a wavenumber from r * (64) to (r + 1) * 64 - 1. `truncation`: equal at latitudes j and 1279 - j.
All inputs are finite; a program needn't handle non-finite values.
Results may differ from the reference program's by a relative error of at most 0.02.
Values may be sent and summed in bfloat16 or wider, within the bound.
A program may use at most 192 MiB of HBM per device.

```python
import math
import jax
import jax.numpy as jnp
from jax import lax

M = 1280
NLAT = 1280
LEV = 8
NLON = 2560
COMP = 8
MW = 20
N_LEV = 8


def draw_wave_order(key, part):
    key = jax.random.fold_in(key, 11)
    wave_count = M // MW
    shuffled = jax.random.permutation(key, wave_count).astype(jnp.int32)
    positions = jnp.arange(M, dtype=jnp.int32)
    owner_row = positions // MW
    round_index = positions % MW
    slot_value = shuffled[owner_row]
    turned = jnp.where(round_index % 2 == 0, slot_value, wave_count - 1 - slot_value)
    return (round_index * wave_count + turned).astype(jnp.int32)


def draw_truncation(key, part):
    key = jax.random.fold_in(key, 23)
    half_count = NLAT // 2
    distance = jnp.arange(half_count, dtype=jnp.int32)
    jitter = jax.random.randint(key, (half_count,), 0, M // 16 + 1, dtype=jnp.int32)
    jitter = jnp.where(distance > 0, jitter, 0)
    half_values = jnp.minimum(M // 8 + distance * 2 * M // NLAT + jitter, M)
    return jnp.concatenate([half_values, half_values[::-1]]).astype(jnp.int32)


def block_levels(rng, extent, split, least, top_value):
    factor_of = 1.0
    for position, shards_of in split:
        heights = jax.random.uniform(jax.random.fold_in(jax.random.fold_in(rng, 6), position), (shards_of,), jnp.float32, least / len(split), top_value / len(split))
        factor_of = factor_of * jnp.repeat(jnp.exp(heights), extent[position] // shards_of).reshape((-1,) + (1,) * (len(extent) - 1 - position))
    return factor_of


def bell_draw(own_key, dims, width, limit, cuts=(), kind=jnp.bfloat16):
    values = width * jax.random.normal(own_key, dims, jnp.float32)
    if cuts:
        values = values * block_levels(own_key, dims, cuts, -0.22, 0.18)
    return jnp.clip(values, -limit, limit).astype(kind)


def setup_inputs(seed: int = 0) -> dict:
    splits = jax.random.split(jax.random.key(seed), 4)
    return {
        "spectra": bell_draw(splits[0], (LEV, M, COMP, M), (M * M) ** -0.5, 0.0048828125, ((0, 8), (1, 64))),
        "wave_order": draw_wave_order(jax.random.fold_in(splits[3], 71), 0),
        "truncation": draw_truncation(jax.random.fold_in(splits[3], 71), 0),
    }


unroll_length = 64
rescale_every = 8

def diagonal_logs(top_wave):
    counts_j = jnp.arange(1, top_wave, dtype=jnp.int32).astype(jnp.float32)
    log_terms = jnp.log((2.0 * counts_j + 1.0) / (2.0 * counts_j))
    summed = jnp.concatenate([jnp.zeros((1,), jnp.float32), jnp.cumsum(log_terms)])
    return 0.5 * math.log(0.5) + 0.5 * summed

def legendre_table(wavenums, latitudes, count_k, lat_count, top_wave):
    log_table = diagonal_logs(top_wave)
    picker = wavenums[:, None] == jnp.arange(top_wave, dtype=jnp.int32)[None, :]
    row_logs = lax.optimization_barrier(jnp.sum(jnp.where(picker, log_table[None, :], jnp.float32(0.0)), axis=1))
    order_m = wavenums.astype(jnp.float32)[:, None]
    angles = math.pi / lat_count * (latitudes.astype(jnp.float32) + 0.5)
    cosine = jnp.cos(angles)[None, :]
    sines = jnp.sin(angles)[None, :]
    grid_shape = (wavenums.shape[0], latitudes.shape[0])
    scale_log = jnp.broadcast_to(row_logs[:, None] + order_m * jnp.log(sines), grid_shape)
    previous = jnp.zeros(grid_shape, jnp.float32)
    current = jnp.ones(grid_shape, jnp.float32)

    def advance(carry, block_index):
        previous, current, scale_log = carry
        outputs = []
        for unroll_step in range(unroll_length):
            degree_k = block_index * unroll_length + unroll_step
            kept_mask = wavenums[:, None] + degree_k < top_wave
            outputs.append(jnp.where(kept_mask, current * jnp.exp(scale_log), jnp.float32(0.0)).astype(jnp.bfloat16))
            next_k = (degree_k + 1).astype(jnp.float32)
            degree = order_m + next_k
            coef_alpha = jnp.sqrt((4.0 * degree * degree - 1.0) / (next_k * (degree + order_m)))
            lower_degree = degree - 1.0
            coef_beta = jnp.sqrt((next_k - 1.0) * (next_k - 1.0 + 2.0 * order_m) / jnp.maximum(4.0 * lower_degree * lower_degree - 1.0, 1.0))
            fresh_value = coef_alpha * (cosine * current - coef_beta * previous)
            previous, current = (current, fresh_value)
            if unroll_step % rescale_every == rescale_every - 1:
                rescale = jnp.maximum(jnp.abs(previous), jnp.abs(current))
                previous = previous / rescale
                current = current / rescale
                scale_log = scale_log + jnp.log(rescale)
        return ((previous, current, scale_log), jnp.stack(outputs))
    block_ids = jnp.arange(count_k // unroll_length, dtype=jnp.int32)
    carried, stacked = lax.scan(advance, (previous, current, scale_log), block_ids)
    return stacked.reshape(count_k, grid_shape[0], grid_shape[1])

def make_dft(wavenums, lon_count):
    phases = wavenums[:, None] * jnp.arange(lon_count, dtype=jnp.int32)[None, :] % lon_count
    angles = phases.astype(jnp.float32) * (2.0 * math.pi / lon_count)
    wave_factor = jnp.where(wavenums == 0, 1.0, 2.0).astype(jnp.float32)[:, None]
    return jnp.stack([wave_factor * jnp.cos(angles), -wave_factor * jnp.sin(angles)]).astype(jnp.bfloat16)

def direct_factor(wavenums, band_lats, kept_mask, lat_count, lon_count, top_wave):
    angles = math.pi / lat_count * (band_lats.astype(jnp.float32) + 0.5)
    lat_weight = float(top_wave) / lon_count * (math.pi / lat_count * jnp.sin(angles))
    wave_factor = jnp.where(wavenums == 0, 1.0, 2.0).astype(jnp.float32)
    return jnp.where(kept_mask, lat_weight[None, :] / (wave_factor * wave_factor)[:, None], jnp.float32(0.0))

def grid_section(banded, wavenums, band_lats, truncation, dft_table, lat_count):
    lev_dev, top_wave, comp_count, band_size = banded.shape
    field_count = comp_count // 2
    lon_count = dft_table.shape[2]
    picker = band_lats[:, None] == jnp.arange(lat_count, dtype=jnp.int32)[None, :]
    band_trunc = lax.optimization_barrier(jnp.sum(jnp.where(picker, truncation[None, :], 0), axis=1))
    kept_mask = wavenums[:, None] < band_trunc[None, :]
    masked = banded.astype(jnp.float32).reshape(lev_dev, top_wave, 2, field_count, band_size) * kept_mask.astype(jnp.float32)[None, :, None, None, :]
    table_wide = dft_table.astype(jnp.float32)
    grid_values = jnp.einsum('liafj,aix->lfjx', masked, table_wide)
    fluxes = jnp.stack([grid_values[:, 0] * grid_values[:, 2], grid_values[:, 1] * grid_values[:, 2], grid_values[:, 0] * grid_values[:, 3], grid_values[:, 1] * grid_values[:, 3]], axis=1).astype(jnp.bfloat16)
    raw_terms = jnp.einsum('lfjx,aix->liafj', fluxes.astype(jnp.float32), table_wide)
    factor = direct_factor(wavenums, band_lats, kept_mask, lat_count, lon_count, top_wave)
    return (raw_terms * factor[None, :, None, None, :]).reshape(lev_dev, top_wave, comp_count, band_size).astype(jnp.bfloat16)

def reference(spectra, wave_order, truncation):
    levels, top_wave, comp_count, count_k = spectra.shape
    lat_count = truncation.shape[0]
    all_lats = jnp.arange(lat_count, dtype=jnp.int32)
    row_block = 64
    block_count = top_wave // row_block
    wave_blocks = wave_order.reshape(block_count, row_block)
    spec_blocks = jnp.moveaxis(spectra.reshape(levels, block_count, row_block, comp_count, count_k), 1, 0)

    def inverse(packed):
        wavenums, spec_block = packed
        legendre = legendre_table(wavenums, all_lats, count_k, lat_count, top_wave)
        return jnp.einsum('lick,kip->licp', spec_block.astype(jnp.float32), legendre.astype(jnp.float32)).astype(jnp.bfloat16)
    fourier = lax.map(inverse, (wave_blocks, spec_blocks))
    fourier = jnp.moveaxis(fourier, 0, 1).reshape(levels, top_wave, comp_count, lat_count)
    dft_table = make_dft(wave_order, NLON)

    def per_level(level_four):
        return grid_section(level_four[None], wave_order, all_lats, truncation, dft_table, lat_count)[0]
    back = lax.map(per_level, fourier)
    back_blocks = jnp.moveaxis(back.reshape(levels, block_count, row_block, comp_count, lat_count), 1, 0)
    lat_group = lat_count // N_LEV

    def direct(packed):
        wavenums, coeff_block = packed
        legendre = legendre_table(wavenums, all_lats, count_k, lat_count, top_wave)
        split_table = legendre.astype(jnp.float32).reshape(count_k, row_block, N_LEV, lat_group)
        split_coeffs = coeff_block.astype(jnp.float32).reshape(levels, row_block, comp_count, N_LEV, lat_group)
        partial_value = jnp.einsum('licbp,kibp->blick', split_coeffs, split_table)
        rounded = lax.optimization_barrier(partial_value.astype(jnp.bfloat16))
        return lax.optimization_barrier(jnp.sum(rounded.astype(jnp.float32), axis=0))
    result = lax.map(direct, (wave_blocks, back_blocks))
    return jnp.moveaxis(result, 0, 1).reshape(levels, top_wave, comp_count, count_k)
```

```python
import functools
import math

import jax
import jax.numpy as jnp
from jax import lax
from jax.experimental import pallas as pl
from jax.experimental.pallas import tpu as pltpu
from jax.sharding import PartitionSpec as P

MESH = pl.DeviceIdType.MESH
F32 = jnp.float32
BF16 = jnp.bfloat16

TOP = 1280
LON = 2560
ROWS = 20
ROWS_PAD = 24
WAVES = 64
LEVS = 8
LANES = 128
RESCALE = 16
GROUPS = ROWS // 2
WIDTHS = tuple(TOP - LANES * g for g in range(GROUPS))
TAB_LEN = (1280, 768, 256)
TAB_STRIDE = (1288, 776, 264)
COLS = WAVES * ROWS_PAD
XROWS = 672
XPAD = 768
XBLK = 112
JBLK = 8


def iota(shape, dim):
    return lax.broadcasted_iota(jnp.int32, shape, dim)


def first_latitude(lev):
    return 64 * lev + jnp.where(lev >= 6, 64, 0)


def half_angles(lat0):
    lat = iota((8, LANES), 1) + lat0
    return math.pi / TOP * (lat.astype(F32) + 0.5)


def own_orders(wo_ref, base):
    rows = iota((ROWS_PAD, LANES), 0)
    orders = jnp.full((ROWS_PAD, LANES), TOP, jnp.int32)
    for r in range(ROWS):
        orders = jnp.where(rows == r, wo_ref[base + r], orders)
    return orders


def recurrence_start(orders, lat0, alpha_ref, both_ref):
    place = iota((16, LANES), 0) * LANES + iota((16, LANES), 1)
    j = jnp.maximum(place, 1).astype(F32)
    terms = jnp.where((place >= 1) & (place < TOP), jnp.log((2.0 * j + 1.0) / (2.0 * j)), 0.0)
    rows = iota((ROWS_PAD, LANES), 0)
    logs = jnp.zeros((ROWS_PAD, LANES), F32)
    for r in range(ROWS):
        part = jnp.where(place <= orders[r : r + 1, 0:1], terms, 0.0)
        total = jnp.sum(jnp.sum(part, axis=0, keepdims=True), axis=1, keepdims=True)
        logs = jnp.where(rows == r, total, logs)
    order = orders.astype(F32)
    angles = half_angles(lat0)
    cosine = jnp.cos(angles)
    log_sine = jnp.log(jnp.sin(angles))
    for kb in range(TOP // LANES):
        k = iota((ROWS_PAD, LANES), 1) + (kb * LANES + 1)
        kf = k.astype(F32)
        n = order + kf
        alpha = jnp.sqrt((4.0 * n * n - 1.0) / (kf * (n + order)))
        low = n - 1.0
        beta = jnp.sqrt(
            (kf - 1.0) * (kf - 1.0 + 2.0 * order) / jnp.maximum(4.0 * low * low - 1.0, 1.0)
        )
        kept = orders + k < TOP
        alpha_ref[kb] = jnp.where(kept, alpha, 0.0)
        both_ref[kb] = jnp.where(kept, alpha * beta, 0.0)
    state = []
    for g in range(3):
        part = slice(8 * g, 8 * g + 8)
        scale = 0.5 * math.log(0.5) + 0.5 * logs[part] + order[part] * log_sine
        state += [jnp.zeros((8, LANES), F32), jnp.ones((8, LANES), F32), scale]
    return cosine, state


def recurrence_phase(phase, cosine, state, alpha_ref, both_ref, tabs):
    live, start, stop = ((3, 0, 2), (2, 2, 6), (1, 6, 10))[phase]

    def block(kb, flat):
        st = [tuple(flat[3 * g : 3 * g + 3]) for g in range(live)]
        alpha = alpha_ref[kb]
        both = both_ref[kb]
        for i in range(LANES):
            if i % RESCALE == 0:
                factor = [jnp.exp(s[2]) for s in st]
            for g in range(live):
                prev, cur, scale = st[g]
                rows = pl.ds(kb * LANES + i, 8, stride=TAB_STRIDE[g])
                tabs[g][rows, :] = cur * factor[g]
                part = slice(8 * g, 8 * g + 8)
                fresh = (alpha[part, i : i + 1] * cosine) * cur - both[part, i : i + 1] * prev
                st[g] = (cur, fresh, scale)
            if i % RESCALE == RESCALE - 1:
                for g in range(live):
                    prev, cur, scale = st[g]
                    big = jnp.maximum(jnp.maximum(jnp.abs(prev), jnp.abs(cur)), 1e-30)
                    inv = 1.0 / big
                    st[g] = (prev * inv, cur * inv, scale + jnp.log(big))
        return tuple(v for s in st for v in s)

    return list(lax.fori_loop(start, stop, block, tuple(state[: 3 * live])))


def table_rows(tabs, r, width):
    g = r // 8
    return tabs[g][pl.ds((r % 8) * TAB_STRIDE[g], width), :].astype(BF16)


def sin_cos(phase):
    turns = jnp.floor(phase * (1.0 / LON))
    phase = phase - turns * LON
    quarter = jnp.floor(phase * (4.0 / LON) + 0.5)
    t = (phase - quarter * (LON // 4)) * (2.0 * math.pi / LON)
    t2 = t * t
    s = t * (1.0 + t2 * (-1.0 / 6 + t2 * (1.0 / 120 + t2 * (-1.0 / 5040 + t2 * (1.0 / 362880)))))
    c = 1.0 + t2 * (-0.5 + t2 * (1.0 / 24 + t2 * (-1.0 / 720 + t2 * (1.0 / 40320))))
    odd = (quarter == 1.0) | (quarter == 3.0)
    sine = jnp.where(odd, c, s)
    cosine = jnp.where(odd, s, c)
    sine = jnp.where((quarter == 2.0) | (quarter == 3.0), -sine, sine)
    cosine = jnp.where((quarter == 1.0) | (quarter == 2.0), -cosine, cosine)
    return sine, cosine


def longitude_tables(mj_ref, cos_xj, sin_xj, cos_jx, sin_jx, even_ref):
    for jb in range(COLS // LANES):
        cols = pl.ds(jb * LANES, LANES)
        mj = mj_ref[:, cols]
        mf = mj.astype(F32)
        live = mj >= 0
        sb, cb = sin_cos(mf * iota((32, LANES), 0).astype(F32))
        sa, ca = sin_cos(mf * (32 * iota((24, LANES), 0)).astype(F32))
        sb = jnp.where(live, sb, 0.0)
        cb = jnp.where(live, cb, 0.0)
        for xa in range(XPAD // 32):
            rows = pl.ds(32 * xa, 32)
            if xa > 20:
                cos_xj[rows, cols] = jnp.zeros((32, LANES), BF16)
                sin_xj[rows, cols] = jnp.zeros((32, LANES), BF16)
                continue
            sa1, ca1 = sa[xa : xa + 1], ca[xa : xa + 1]
            c = ca1 * cb - sa1 * sb
            s = sa1 * cb + ca1 * sb
            if xa == 20:
                c = jnp.where(iota((32, LANES), 0) == 0, c, 0.0)
                s = jnp.where(iota((32, LANES), 0) == 0, s, 0.0)
            cos_xj[rows, cols] = c.astype(BF16)
            sin_xj[rows, cols] = s.astype(BF16)
        even = jnp.where(lax.rem(mj, 2) == 0, 1.0, 0.0)
        even_ref[cols, :] = jnp.broadcast_to(even, (LANES, LANES)).T
        for xb in range(XPAD // LANES):
            rows = pl.ds(xb * LANES, LANES)
            cos_jx[cols, rows] = cos_xj[rows, cols].T
            sin_jx[cols, rows] = sin_xj[rows, cols].T


def pick_fields():
    row, col = iota((256, 512), 0), iota((256, 512), 1)
    slot, s, l, part, field = row // 128, row // 64 % 2, row // 8 % 8, row // 4 % 2, row % 4
    c_part, side, c_slot = col // 256, col // 128 % 2, col // 64 % 2
    flux, c_s, c_l = col // 16 % 4, col // 8 % 2, col % 8
    wanted = jnp.where(side == 0, flux % 2, 2 + flux // 2)
    same = (slot == c_slot) & (s == c_s) & (l == c_l) & (part == c_part) & (field == wanted)
    return jnp.where(same, 1.0, 0.0).astype(BF16)


def place_fluxes():
    row, col = iota((256, 256), 0), iota((256, 256), 1)
    part, slot, flux, s, l = row // 128, row // 64 % 2, row // 16 % 4, row // 8 % 2, row % 8
    same = (slot == col // 128) & (s == col // 64 % 2) & (l == col // 8 % 8)
    same = same & (part == col // 4 % 2) & (flux == col % 4)
    return jnp.where(same, 1.0, 0.0).astype(BF16)


def kernel(
    wo_ref, trunc_ref, mj_ref, spec_ref, out_ref,
    alpha_ref, both_ref, tab0, tab1, tab2,
    cos_xj, sin_xj, cos_jx, sin_jx, even_ref,
    gath, stage, send_f, recv_f, send_b, recv_b,
    x_re, x_im, h_c, h_s,
    partial, e1_recv, e2_send, e2_recv,
    own_sem, g_send, g_recv, c_send, c_recv, f_ss, f_rs, b_ss, b_rs, e1_ss, e1_rs, e2_ss, e2_rs,
):
    me = lax.axis_index("wave")
    lev = lax.axis_index("lev")
    y = lev // 2
    core = lev % 2
    partner = y * 2 + (1 - core)
    two = (lev == 5) | (lev == 7)
    tabs = (tab0, tab1, tab2)

    recv_f[...] = jnp.zeros_like(recv_f)
    recv_b[...] = jnp.zeros_like(recv_b)

    barrier = pltpu.get_barrier_semaphore()

    @pl.loop(1, WAVES)
    def _(i):
        pl.semaphore_signal(
            barrier, inc=1, device_id=(lax.rem(me + i, WAVES), lev), device_id_type=MESH
        )

    for i in range(1, 4):
        pl.semaphore_signal(
            barrier, inc=1, device_id=(me, lax.rem(lev + 2 * i, LEVS)), device_id_type=MESH
        )
    pl.semaphore_signal(barrier, inc=1, device_id=(me, partner), device_id_type=MESH)

    longitude_tables(mj_ref, cos_xj, sin_xj, cos_jx, sin_jx, even_ref)
    lat0 = first_latitude(lev)
    orders = own_orders(wo_ref, me * ROWS)
    cosine, state = recurrence_start(orders, lat0, alpha_ref, both_ref)

    pl.semaphore_wait(barrier, WAVES - 1 + 4)

    def piece(ref, level, g):
        return ref.at[level, pl.ds(2 * g, 2), :, pl.ds(0, WIDTHS[g])]

    def own_copy():
        return pltpu.make_async_copy(spec_ref.at[0], gath.at[lev], own_sem)

    def y_copy(i, g):
        return pltpu.make_async_remote_copy(
            piece(spec_ref, 0, g), piece(gath, lev, g), g_send.at[i, g], g_recv.at[i, g],
            device_id=(me, lax.rem(lev + 2 * i, LEVS)), device_id_type=MESH,
        )

    def core_copy(i, g):
        level = lax.rem(lev + LEVS - 2 * i, LEVS)
        src = piece(spec_ref, 0, g) if i == 0 else piece(gath, level, g)
        return pltpu.make_async_remote_copy(
            src, piece(gath, level, g), c_send.at[i, g], c_recv.at[i, g],
            device_id=(me, partner), device_id_type=MESH,
        )

    own_copy().start()
    for g in range(GROUPS):
        for i in range(1, 4):
            y_copy(i, g).start()
    for g in range(GROUPS):
        core_copy(0, g).start()

    state = recurrence_phase(0, cosine, state, alpha_ref, both_ref, tabs)
    state = recurrence_phase(1, cosine, state, alpha_ref, both_ref, tabs)
    for g in range(GROUPS):
        for i in range(1, 4):
            y_copy(i, g).wait()
            core_copy(i, g).start()
    recurrence_phase(2, cosine, state, alpha_ref, both_ref, tabs)
    own_copy().wait()
    for g in range(GROUPS):
        for i in range(4):
            core_copy(i, g).wait()

    angles = half_angles(lat0)[0:1]
    unit = lat0 // 64
    low_row = trunc_ref[pl.ds(unit // 2, 1), :]
    high_row = trunc_ref[pl.ds(unit // 2 + 1, 1), :]
    split = jnp.concatenate([low_row[:, 64:], high_row[:, :64]], axis=1)
    cut = jnp.where(unit % 2 == 0, low_row, split)
    area = (float(TOP) / LON) * (math.pi / TOP) * jnp.sin(angles)
    sign = jnp.where(iota((1, TOP), 1) % 2 == 0, 1.0, -1.0)

    stage[...] = jnp.zeros_like(stage)
    for r in range(ROWS):
        width = WIDTHS[r // 2]
        table = table_rows(tabs, r, width)
        coeff = gath[:, r, :, 0:width].astype(F32).reshape(64, width)
        both_signs = jnp.concatenate([coeff, coeff * sign[:, :width]], axis=0).astype(BF16)
        fourier = jnp.dot(both_signs, table, preferred_element_type=F32)
        order = wo_ref[me * ROWS + r]
        weight = jnp.where(order == 0, 1.0, 2.0)
        fourier = fourier * jnp.where(order < cut, weight, 0.0)
        stage[pl.ds(r, LANES, stride=ROWS_PAD), :] = fourier.T

    def f_copy(i, count):
        to = lax.rem(me + i, WAVES)
        return pltpu.make_async_remote_copy(
            send_f.at[to, pl.ds(0, count)], recv_f.at[me, pl.ds(0, count)], f_ss.at[i], f_rs.at[i],
            device_id=(to, lev), device_id_type=MESH,
        )

    def b_copy(i, count):
        to = lax.rem(me + i, WAVES)
        return pltpu.make_async_remote_copy(
            send_b.at[to, pl.ds(0, count)], recv_b.at[me, pl.ds(0, count)], b_ss.at[i], b_rs.at[i],
            device_id=(to, lev), device_id_type=MESH,
        )

    def each_width(act):
        @pl.when(two)
        def _():
            act(2)

        @pl.when(jnp.logical_not(two))
        def _():
            act(1)

    @pl.loop(0, WAVES)
    def _(i):
        to = lax.rem(me + i, WAVES)
        for slot in range(2):
            rows = pl.ds(pl.multiple_of((slot * WAVES + to) * ROWS_PAD, 8), ROWS_PAD)
            send_f[to, slot] = stage[rows, :].astype(BF16)

        @pl.when(i > 0)
        def _():
            each_width(lambda count: f_copy(i, count).start())

    recv_f[me] = send_f[me]

    h_c[pl.ds(XROWS, XPAD - XROWS), :] = jnp.zeros((XPAD - XROWS, 256), BF16)
    h_s[pl.ds(XROWS, XPAD - XROWS), :] = jnp.zeros((XPAD - XROWS, 256), BF16)

    @pl.loop(1, WAVES)
    def _(i):
        each_width(lambda count: f_copy(i, count).wait())

    fields = pick_fields()

    @pl.loop(0, WAVES // JBLK)
    def _(b):
        rows = pl.ds(pl.multiple_of(b * JBLK * ROWS_PAD, 64), JBLK * ROWS_PAD)
        raw = recv_f[pl.ds(b * JBLK, JBLK)].astype(F32)
        flat = [raw[:, slot].reshape(JBLK * ROWS_PAD, LANES) for slot in range(2)]
        raw = jnp.concatenate(flat, axis=1).astype(BF16)
        picked = jnp.dot(raw, fields, preferred_element_type=F32)
        even = even_ref[rows, :]
        even = jnp.concatenate([even, even], axis=1)
        for part, ref in ((0, x_re), (1, x_im)):
            both = picked[:, 256 * part : 256 * part + 256]
            evens = both * even
            ref[rows, :] = jnp.concatenate([evens, both - evens], axis=1).astype(BF16)

    @pl.loop(0, XROWS // XBLK)
    def _(b):
        rows = pl.ds(pl.multiple_of(b * XBLK, 16), XBLK)
        c = jnp.dot(cos_xj[rows, :], x_re[...], preferred_element_type=F32)
        s = jnp.dot(sin_xj[rows, :], x_im[...], preferred_element_type=F32)
        c_sum, c_dif = c[:, :256] + c[:, 256:], c[:, :256] - c[:, 256:]
        s_sum, s_dif = s[:, :256] + s[:, 256:], s[:, :256] - s[:, 256:]

        def flux(g):
            return g[:, :128] * g[:, 128:]

        x = iota((XBLK, LANES), 0) + b * XBLK
        once = jnp.where((x == 0) | (x == LON // 4), 0.5, 1.0)
        f1 = flux(c_sum - s_sum) * once
        f2 = flux(c_sum + s_sum) * once
        f3 = flux(c_dif + s_dif) * once
        f4 = flux(c_dif - s_dif) * once
        near, far = f1 + f2, f3 + f4
        near_d, far_d = f2 - f1, f3 - f4
        h_c[rows, :] = jnp.concatenate([near + far, near - far], axis=1).astype(BF16)
        h_s[rows, :] = jnp.concatenate([near_d + far_d, near_d - far_d], axis=1).astype(BF16)

    places = place_fluxes()

    @pl.loop(0, WAVES // JBLK)
    def _(b):
        block = lax.rem(me // JBLK + b, WAVES // JBLK)
        rows = pl.ds(pl.multiple_of(block * JBLK * ROWS_PAD, 64), JBLK * ROWS_PAD)
        c = jnp.dot(cos_jx[rows, :], h_c[...], preferred_element_type=F32)
        s = jnp.dot(sin_jx[rows, :], h_s[...], preferred_element_type=F32)
        even = even_ref[rows, :] > 0.5
        c = jnp.where(even, c[:, :128], c[:, 128:])
        s = jnp.where(even, s[:, :128], s[:, 128:])
        back = jnp.dot(
            jnp.concatenate([c, s], axis=1).astype(BF16), places, preferred_element_type=F32
        )
        for slot in range(2):
            part = back[:, 128 * slot : 128 * slot + 128].reshape(JBLK, ROWS_PAD, LANES)
            send_b[pl.ds(block * JBLK, JBLK), slot] = part.astype(BF16)

        @pl.loop(0, JBLK)
        def _(n):
            to = block * JBLK + n
            i = lax.rem(to - me + WAVES, WAVES)

            @pl.when(i > 0)
            def _():
                each_width(lambda count: b_copy(i, count).start())

    recv_b[me] = send_b[me]

    @pl.loop(1, WAVES)
    def _(i):
        each_width(lambda count: b_copy(i, count).wait())

    @pl.loop(0, WAVES)
    def _(w):
        for slot in range(2):
            rows = pl.ds(pl.multiple_of((slot * WAVES + w) * ROWS_PAD, 8), ROWS_PAD)
            stage[rows, :] = recv_b[w, slot].astype(F32)

    def e1_copy(g):
        window = (slice(None), pl.ds(2 * g, 2), slice(None), pl.ds(0, WIDTHS[g]))
        return pltpu.make_async_remote_copy(
            partial.at[(1 - core,) + window], e1_recv.at[window], e1_ss.at[g], e1_rs.at[g],
            device_id=(me, partner), device_id_type=MESH,
        )

    def e2_copy(i, g):
        to_y = lax.rem(y + i, 4)
        return pltpu.make_async_remote_copy(
            piece(e2_send, to_y, g), piece(e2_recv, y, g), e2_ss.at[i, g], e2_rs.at[i, g],
            device_id=(me, to_y * 2 + core), device_id_type=MESH,
        )

    def forward(g):
        e1_copy(g).wait()
        for r in (2 * g, 2 * g + 1):
            for q in range(4):
                mine = partial[core, q, r, :, 0 : WIDTHS[g]].astype(F32)
                other = e1_recv[q, r, :, 0 : WIDTHS[g]].astype(F32)
                e2_send[q, r, :, 0 : WIDTHS[g]] = (mine + other).astype(BF16)
        for i in range(1, 4):
            e2_copy(i, g).start()

    for g in range(GROUPS):
        width = WIDTHS[g]
        for r in (2 * g, 2 * g + 1):
            table = table_rows(tabs, r, width)
            order = wo_ref[me * ROWS + r]
            weight = jnp.where(order == 0, 1.0, 0.5)
            factor = jnp.where(order < cut, area * weight, 0.0)
            back = stage[pl.ds(r, LANES, stride=ROWS_PAD), :].T * factor
            sums = lax.dot_general(
                back.astype(BF16), table, (((1,), (1,)), ((), ())), preferred_element_type=F32
            )
            sums = sums[:64] + sums[64:] * sign[:, :width]
            for l in range(LEVS):
                partial[l % 2, l // 2, r, :, 0:width] = sums[8 * l : 8 * l + 8].astype(BF16)
        e1_copy(g).start()
        if g > 0:
            forward(g - 1)
    forward(GROUPS - 1)
    for g in range(GROUPS):
        width = WIDTHS[g]
        for i in range(1, 4):
            e2_copy(i, g).wait()
        for r in (2 * g, 2 * g + 1):
            total = e2_send[y, r, :, 0:width].astype(F32)
            for i in range(1, 4):
                total = total + e2_recv[lax.rem(y + i, 4), r, :, 0:width].astype(F32)
            out_ref[0, r, :, 0:width] = total
            if width < TOP:
                out_ref[0, r, :, width:TOP] = jnp.zeros((8, TOP - width), F32)


def on_device(spectra, wave_order, truncation):
    mj = jnp.pad(wave_order.reshape(WAVES, ROWS), ((0, 0), (0, ROWS_PAD - ROWS)), constant_values=-1)
    vmem = pl.BlockSpec(memory_space=pltpu.VMEM)
    dma = pltpu.SemaphoreType.DMA
    return pl.pallas_call(
        kernel,
        out_shape=jax.ShapeDtypeStruct((1, ROWS, 8, TOP), F32),
        in_specs=[
            pl.BlockSpec(memory_space=pltpu.SMEM), vmem, vmem, pl.BlockSpec(memory_space=pl.ANY),
        ],
        out_specs=vmem,
        scratch_shapes=[
            pltpu.VMEM((10, ROWS_PAD, LANES), F32),
            pltpu.VMEM((10, ROWS_PAD, LANES), F32),
            pltpu.VMEM((8 * TAB_STRIDE[0], LANES), F32),
            pltpu.VMEM((8 * TAB_STRIDE[1], LANES), F32),
            pltpu.VMEM((8 * TAB_STRIDE[2], LANES), F32),
            pltpu.VMEM((XPAD, COLS), BF16),
            pltpu.VMEM((XPAD, COLS), BF16),
            pltpu.VMEM((COLS, XPAD), BF16),
            pltpu.VMEM((COLS, XPAD), BF16),
            pltpu.VMEM((COLS, LANES), F32),
            pltpu.VMEM((LEVS, ROWS, 8, TOP), BF16),
            pltpu.VMEM((2 * COLS, LANES), F32),
            pltpu.VMEM((WAVES, 2, ROWS_PAD, LANES), BF16),
            pltpu.VMEM((WAVES, 2, ROWS_PAD, LANES), BF16),
            pltpu.VMEM((WAVES, 2, ROWS_PAD, LANES), BF16),
            pltpu.VMEM((WAVES, 2, ROWS_PAD, LANES), BF16),
            pltpu.VMEM((COLS, 512), BF16),
            pltpu.VMEM((COLS, 512), BF16),
            pltpu.VMEM((XPAD, 256), BF16),
            pltpu.VMEM((XPAD, 256), BF16),
            pltpu.VMEM((2, 4, ROWS, 8, TOP), BF16),
            pltpu.VMEM((4, ROWS, 8, TOP), BF16),
            pltpu.VMEM((4, ROWS, 8, TOP), BF16),
            pltpu.VMEM((4, ROWS, 8, TOP), BF16),
            dma,
            dma((4, GROUPS)), dma((4, GROUPS)), dma((4, GROUPS)), dma((4, GROUPS)),
            dma((WAVES,)), dma((WAVES,)), dma((WAVES,)), dma((WAVES,)),
            dma((GROUPS,)), dma((GROUPS,)), dma((4, GROUPS)), dma((4, GROUPS)),
        ],
        compiler_params=pltpu.CompilerParams(
            collective_id=0, has_side_effects=True, vmem_limit_bytes=60 * 2**20
        ),
        name="flux_transform",
    )(wave_order, truncation.reshape(10, LANES), mj.reshape(1, COLS), spectra)


def solution(mesh):
    return jax.shard_map(
        on_device,
        mesh=mesh,
        in_specs=(P("lev", "wave", None, None), P(), P()),
        out_specs=P("lev", "wave", None, None),
        check_vma=False,
    )
```

```python
import functools
import math

import jax
import jax.numpy as jnp
from jax import lax
from jax.experimental import pallas as pl
from jax.experimental.pallas import tpu as pltpu
from jax.sharding import PartitionSpec as P

MESH = pl.DeviceIdType.MESH
F32 = jnp.float32
BF16 = jnp.bfloat16

TOP = 1280
LON = 2560
ROWS = 20
ROWS_PAD = 24
LIGHT = 12
HEAVY = 8
WAVES = 64
LEVS = 8
LANES = 128
RESCALE = 16
GROUPS = ROWS // 2
WIDTHS = tuple(TOP - LANES * g for g in range(GROUPS))
TAB_LEN = (1280, 768, 256)
TAB_STRIDE = (1288, 776, 264)
COLS = WAVES * ROWS
LIGHT_COLS = WAVES * LIGHT
XROWS = 672
XPAD = 768
XBLK = 112
TILE = 4
UP = (0, 3, 4, 7, 8)


def iota(shape, dim):
    return lax.broadcasted_iota(jnp.int32, shape, dim)


def first_latitude(lev):
    return 160 * (lev // 2) + 64 * (lev % 2)


def half_angles(lat0):
    lat = iota((8, LANES), 1) + lat0
    return math.pi / TOP * (lat.astype(F32) + 0.5)


def own_orders(wo_ref, base):
    rows = iota((ROWS_PAD, LANES), 0)
    orders = jnp.full((ROWS_PAD, LANES), TOP, jnp.int32)
    for r in range(ROWS):
        orders = jnp.where(rows == r, wo_ref[base + r], orders)
    return orders


def recurrence_start(wo_ref, base, orders, lat0, alpha_ref, both_ref):
    place = iota((16, LANES), 0) * LANES + iota((16, LANES), 1)
    j = jnp.maximum(place, 1).astype(F32)
    terms = jnp.where((place >= 1) & (place < TOP), jnp.log((2.0 * j + 1.0) / (2.0 * j)), 0.0)
    rows = iota((ROWS_PAD, LANES), 0)
    logs = jnp.zeros((ROWS_PAD, LANES), F32)
    for r in range(ROWS):
        part = jnp.where(place <= wo_ref[base + r], terms, 0.0)
        total = jnp.sum(jnp.sum(part, axis=0, keepdims=True), axis=1, keepdims=True)
        logs = jnp.where(rows == r, total, logs)
    order = orders.astype(F32)
    angles = half_angles(lat0)
    cosine = jnp.cos(angles)
    log_sine = jnp.log(jnp.sin(angles))
    for kb in range(TOP // LANES):
        k = iota((ROWS_PAD, LANES), 1) + (kb * LANES + 1)
        kf = k.astype(F32)
        n = order + kf
        alpha = jnp.sqrt((4.0 * n * n - 1.0) / (kf * (n + order)))
        low = n - 1.0
        beta = jnp.sqrt(
            (kf - 1.0) * (kf - 1.0 + 2.0 * order) / jnp.maximum(4.0 * low * low - 1.0, 1.0)
        )
        kept = orders + k < TOP
        alpha_ref[kb] = jnp.where(kept, alpha, 0.0)
        both_ref[kb] = jnp.where(kept, alpha * beta, 0.0)
    state = []
    for g in range(3):
        part = slice(8 * g, 8 * g + 8)
        scale = 0.5 * math.log(0.5) + 0.5 * logs[part] + order[part] * log_sine
        state += [jnp.zeros((8, LANES), F32), jnp.ones((8, LANES), F32), scale]
    return cosine, state


def recurrence_phase(phase, cosine, state, alpha_ref, both_ref, tabs):
    live, start, stop = ((3, 0, 2), (2, 2, 6), (1, 6, 10))[phase]

    def block(kb, flat):
        st = [tuple(flat[3 * g : 3 * g + 3]) for g in range(live)]
        alpha = alpha_ref[kb]
        both = both_ref[kb]
        for i in range(LANES):
            if i % RESCALE == 0:
                factor = [jnp.exp(s[2]) for s in st]
            for g in range(live):
                prev, cur, scale = st[g]
                rows = pl.ds(kb * LANES + i, 8, stride=TAB_STRIDE[g])
                tabs[g][rows, :] = cur * factor[g]
                part = slice(8 * g, 8 * g + 8)
                fresh = (alpha[part, i : i + 1] * cosine) * cur - both[part, i : i + 1] * prev
                st[g] = (cur, fresh, scale)
            if i % RESCALE == RESCALE - 1:
                for g in range(live):
                    prev, cur, scale = st[g]
                    big = jnp.maximum(jnp.maximum(jnp.abs(prev), jnp.abs(cur)), 1e-30)
                    inv = 1.0 / big
                    st[g] = (prev * inv, cur * inv, scale + jnp.log(big))
        return tuple(v for s in st for v in s)

    return list(lax.fori_loop(start, stop, block, tuple(state[: 3 * live])))


def table_rows(tabs, r, width):
    g = r // 8
    return tabs[g][pl.ds((r % 8) * TAB_STRIDE[g], width), :].astype(BF16)


def sin_cos(phase):
    turns = jnp.floor(phase * (1.0 / LON))
    phase = phase - turns * LON
    quarter = jnp.floor(phase * (4.0 / LON) + 0.5)
    t = (phase - quarter * (LON // 4)) * (2.0 * math.pi / LON)
    t2 = t * t
    s = t * (1.0 + t2 * (-1.0 / 6 + t2 * (1.0 / 120 + t2 * (-1.0 / 5040 + t2 * (1.0 / 362880)))))
    c = 1.0 + t2 * (-0.5 + t2 * (1.0 / 24 + t2 * (-1.0 / 720 + t2 * (1.0 / 40320))))
    odd = (quarter == 1.0) | (quarter == 3.0)
    sine = jnp.where(odd, c, s)
    cosine = jnp.where(odd, s, c)
    sine = jnp.where((quarter == 2.0) | (quarter == 3.0), -sine, sine)
    cosine = jnp.where((quarter == 1.0) | (quarter == 2.0), -cosine, cosine)
    return sine, cosine


def longitude_tables(mt_ref, cos_xj, sin_xj, cos_jx, sin_jx, even_ref):
    @pl.loop(0, COLS // LANES)
    def _(jb):
        cols = pl.ds(pl.multiple_of(jb * LANES, LANES), LANES)
        mj = mt_ref[pl.ds(jb, 1), :]
        mf = mj.astype(F32)
        sb, cb = sin_cos(mf * iota((32, LANES), 0).astype(F32))
        sa, ca = sin_cos(mf * (32 * iota((24, LANES), 0)).astype(F32))
        for xa in range(XPAD // 32):
            rows = pl.ds(32 * xa, 32)
            if xa > 20:
                cos_xj[rows, cols] = jnp.zeros((32, LANES), BF16)
                sin_xj[rows, cols] = jnp.zeros((32, LANES), BF16)
                continue
            sa1, ca1 = sa[xa : xa + 1], ca[xa : xa + 1]
            c = ca1 * cb - sa1 * sb
            s = sa1 * cb + ca1 * sb
            if xa == 20:
                c = jnp.where(iota((32, LANES), 0) == 0, c, 0.0)
                s = jnp.where(iota((32, LANES), 0) == 0, s, 0.0)
            cos_xj[rows, cols] = c.astype(BF16)
            sin_xj[rows, cols] = s.astype(BF16)
        even = jnp.where(lax.rem(mj, 2) == 0, 1.0, 0.0)
        even_ref[cols, :] = jnp.broadcast_to(even, (LANES, LANES)).T
        for xb in range(XPAD // LANES):
            rows = pl.ds(xb * LANES, LANES)
            cos_jx[cols, rows] = cos_xj[rows, cols].T
            sin_jx[cols, rows] = sin_xj[rows, cols].T


def grid_lane(u):
    slot, v = u // 64, u % 64
    flux = jnp.where(slot == 0, v // 16, v // 8)
    s = jnp.where(slot == 0, v // 8 % 2, v // 4 % 2)
    level = jnp.where(slot == 0, v % 8, v % 4)
    return slot, flux, s, level, (slot == 0) | (v < 32)


def pick_fields():
    row, col = iota((256, 512), 0), iota((256, 512), 1)
    slot, level, s, part, field = row // 128, row // 16 % 8, row // 8 % 2, row // 4 % 2, row % 4
    c_part, side = col // 256, col // 128 % 2
    c_slot, flux, c_s, c_level, used = grid_lane(col % 128)
    wanted = jnp.where(side == 0, flux % 2, 2 + flux // 2)
    same = used & (slot == c_slot) & (s == c_s) & (level == c_level)
    same = same & (part == c_part) & (field == wanted)
    return jnp.where(same, 1.0, 0.0).astype(BF16)


def place_fluxes():
    row, col = iota((256, 256), 0), iota((256, 256), 1)
    part = row // 128
    slot, flux, s, level, used = grid_lane(row % 128)
    c_slot = col // 128
    c_level = jnp.where(c_slot == 0, col // 16 % 8, col // 16 % 4)
    same = used & (slot == c_slot) & (level == c_level) & (s == col // 8 % 2)
    same = same & (part == col // 4 % 2) & (flux == col % 4)
    return jnp.where(same, 1.0, 0.0).astype(BF16)


def kernel(
    wo_ref, mt_ref, spec_ref, out_ref,
    alpha_ref, both_ref, tab0, tab1, tab2,
    cos_xj, sin_xj, cos_jx, sin_jx, even_ref,
    gath, stage_l, stage_h, send_fl, send_fh, recv_fl, recv_fh, send_bl, send_bh, recv_bl, recv_bh,
    flat0, flat1, x_re, x_im, acc_c, acc_s, h_c, h_s,
    partial, e1_recv, e2_send, e2_sum, rel_recv, e2_recv,
    own_sem, g_send, g_recv, r_send, r_recv, c_send, c_recv,
    fl_ss, fl_rs, fh_ss, fh_rs, bl_ss, bl_rs, bh_ss, bh_rs,
    e1_ss, e1_rs, rel_ss, rel_rs, e2_ss, e2_rs, sum_ss, sum_rs,
):
    me = lax.axis_index("wave")
    lev = lax.axis_index("lev")
    y = lev // 2
    core = lev % 2
    partner = y * 2 + (1 - core)
    up = lax.rem(lev + 2, LEVS)
    down = lax.rem(lev + 6, LEVS)
    tabs = (tab0, tab1, tab2)
    lane4 = iota((TILE, LANES), 1)

    barrier = pltpu.get_barrier_semaphore()
    for other in (up, down, partner):
        pl.semaphore_signal(barrier, inc=1, device_id=(me, other), device_id_type=MESH)

    @pl.loop(1, WAVES)
    def _(i):
        pl.semaphore_signal(
            barrier, inc=1, device_id=(lax.rem(me + i, WAVES), lev), device_id_type=MESH
        )

    lat0 = first_latitude(lev)
    orders = own_orders(wo_ref, me * ROWS)
    cosine, state = recurrence_start(wo_ref, me * ROWS, orders, lat0, alpha_ref, both_ref)
    flat0[...] = jnp.zeros_like(flat0)
    flat1[...] = jnp.zeros_like(flat1)
    h_c[pl.ds(XROWS, XPAD - XROWS), :] = jnp.zeros((XPAD - XROWS, 256), BF16)
    h_s[pl.ds(XROWS, XPAD - XROWS), :] = jnp.zeros((XPAD - XROWS, 256), BF16)

    longitude_tables(mt_ref, cos_xj, sin_xj, cos_jx, sin_jx, even_ref)
    pl.semaphore_wait(barrier, WAVES - 1 + 3)

    light_groups = tuple(range(HEAVY // 2, GROUPS))
    heavy_groups = tuple(range(HEAVY // 2))

    def piece(ref, level, g):
        return ref.at[level, pl.ds(2 * g, 2), :, pl.ds(0, WIDTHS[g])]

    def own_copy():
        return pltpu.make_async_copy(spec_ref.at[0], gath.at[lev], own_sem)

    def y_copy(way, g):
        return pltpu.make_async_remote_copy(
            piece(spec_ref, 0, g), piece(gath, lev, g), g_send.at[way, g], g_recv.at[way, g],
            device_id=(me, up if way == 0 else down), device_id_type=MESH,
        )

    def relay_copy(g):
        level = down if g in UP else up
        return pltpu.make_async_remote_copy(
            piece(gath, level, g), piece(gath, level, g), r_send.at[g], r_recv.at[g],
            device_id=(me, up if g in UP else down), device_id_type=MESH,
        )

    def core_copy(i, g):
        level = (lev, down, up, lax.rem(lev + 4, LEVS))[i]
        src = piece(spec_ref, 0, g) if i == 0 else piece(gath, level, g)
        return pltpu.make_async_remote_copy(
            src, piece(gath, level, g), c_send.at[i, g], c_recv.at[i, g],
            device_id=(me, partner), device_id_type=MESH,
        )

    def pass_on(groups):
        for g in groups:
            for way in range(2):
                y_copy(way, g).wait()
            relay_copy(g).start()
            for i in (1, 2):
                core_copy(i, g).start()

    def pass_last(groups):
        for g in groups:
            relay_copy(g).wait()
            core_copy(3, g).start()

    def gathered(groups):
        for g in groups:
            for i in range(4):
                core_copy(i, g).wait()

    for g in light_groups + heavy_groups:
        for way in range(2):
            y_copy(way, g).start()
    own_copy().start()
    for g in light_groups + heavy_groups:
        core_copy(0, g).start()

    angles = half_angles(lat0)[0:1]
    unit = lat0 // 32
    cut_row = COLS // LANES + unit // 4
    wide = jnp.concatenate([mt_ref[pl.ds(cut_row, 1), :], mt_ref[pl.ds(cut_row + 1, 1), :]], axis=1)
    cut = wide[:, 0:LANES]
    for n in range(1, 4):
        cut = jnp.where(unit % 4 == n, wide[:, 32 * n : 32 * n + LANES], cut)
    area = (float(TOP) / LON) * (math.pi / TOP) * jnp.sin(angles)
    area = jnp.where(iota((1, LANES), 1) < 64 + 32 * core, area, 0.0)
    sign = jnp.where(iota((1, TOP), 1) % 2 == 0, 1.0, -1.0)

    def legendre_row(r):
        width = WIDTHS[r // 2]
        table = table_rows(tabs, r, width)
        coeff = gath[:, r, :, 0:width].astype(F32)
        both_signs = jnp.stack([coeff, coeff * sign[:, :width]], axis=1).reshape(LANES, width)
        fourier = jnp.dot(both_signs.astype(BF16), table, preferred_element_type=F32)
        order = wo_ref[me * ROWS + r]
        weight = jnp.where(order == 0, 1.0, 2.0)
        fourier = fourier * jnp.where(order < cut, weight, 0.0)
        if r < HEAVY:
            stage_h[pl.ds(r, LANES, stride=HEAVY), :] = fourier.T
        else:
            stage_l[pl.ds(r - HEAVY, LANES, stride=LIGHT), :] = fourier.T

    def both_cores(main, extra, act):
        @pl.when(core == 0)
        def _():
            act(main)

        @pl.when(core == 1)
        def _():
            act(main + extra)

    def peer_copy(send, recv, ss, rs, i, count):
        to = lax.rem(me + i, WAVES)
        return pltpu.make_async_remote_copy(
            send.at[to, pl.ds(0, count)], recv.at[me, pl.ds(0, count)], ss, rs,
            device_id=(to, lev), device_id_type=MESH,
        )

    def send_all(bufs, main, extra):
        def start(count):
            @pl.loop(1, WAVES, unroll=7)
            def _(i):
                peer_copy(*bufs, i, count).start()

        both_cores(main, extra, start)
        bufs[1][me] = bufs[0][me]

    def wait_all(bufs, main, extra):
        send, recv, ss, rs = bufs

        def wait(count):
            window = (pl.ds(0, WAVES - 1), pl.ds(0, count))
            pltpu.make_async_copy(send.at[window], send.at[window], ss).wait()
            pltpu.make_async_copy(recv.at[window], recv.at[window], rs).wait()

        both_cores(main, extra, wait)

    fl = (send_fl, recv_fl, fl_ss, fl_rs)
    fh = (send_fh, recv_fh, fh_ss, fh_rs)
    bl = (send_bl, recv_bl, bl_ss, bl_rs)
    bh = (send_bh, recv_bh, bh_ss, bh_rs)

    def pack(stage, send, rows, main, extra):
        @pl.loop(0, WAVES, unroll=8)
        def _(w):
            for q in range(main):
                send[w, q] = stage[pl.ds(w * rows + TILE * q, TILE), :].astype(BF16)

        @pl.when(core == 1)
        def _():
            @pl.loop(0, WAVES // 2, unroll=8)
            def _(e):
                base = (WAVES + e) * rows
                for q in range(extra):
                    first = stage[pl.ds(base + TILE * q, TILE), :]
                    second = stage[pl.ds(base + rows // 2 + TILE * q, TILE), :]
                    second = pltpu.roll(second, 64, 1)
                    send[2 * e, main + q] = jnp.where(lane4 < 64, first, second).astype(BF16)
                    send[2 * e + 1, main + q] = jnp.where(lane4 < 64, second, first).astype(BF16)

    recurrence_phase0 = recurrence_phase(0, cosine, state, alpha_ref, both_ref, tabs)
    pass_on(light_groups)
    state = recurrence_phase(1, cosine, recurrence_phase0, alpha_ref, both_ref, tabs)
    pass_last(light_groups)
    pass_on(heavy_groups)
    own_copy().wait()
    gathered(light_groups)

    for r in range(HEAVY, ROWS):
        legendre_row(r)
    pack(stage_l, send_fl, LIGHT, 3, 2)
    send_all(fl, 3, 2)

    recurrence_phase(2, cosine, state, alpha_ref, both_ref, tabs)
    pass_last(heavy_groups)
    gathered(heavy_groups)
    for r in range(HEAVY):
        legendre_row(r)
    pack(stage_h, send_fh, HEAVY, 2, 1)
    send_all(fh, 2, 1)

    fields = pick_fields()

    def unpack(recv, rows, main, extra):
        @pl.loop(0, WAVES, unroll=8)
        def _(d):
            base = d * rows
            for q in range(main):
                flat0[pl.ds(base + TILE * q, TILE), :] = recv[d, q].astype(F32)

        @pl.when(core == 1)
        def _():
            odd = me % 2 == 1

            @pl.loop(0, WAVES, unroll=8)
            def _(d):
                base = d * rows
                later = []
                for q in reversed(range(extra)):
                    here = recv[d, main + q].astype(F32)
                    there = pltpu.roll(here, 64, 1)
                    flat1[pl.ds(base + TILE * q, TILE), :] = jnp.where(odd, there, here)
                    later.append((base + rows // 2 + TILE * q, jnp.where(odd, here, there)))
                for place, value in reversed(later):
                    flat1[pl.ds(place, TILE), :] = value

    def build(first_row, count):
        @pl.loop(0, count // LANES)
        def _(b):
            local = pl.ds(pl.multiple_of(b * LANES, LANES), LANES)
            rows = pl.ds(pl.multiple_of(first_row + b * LANES, LANES), LANES)
            raw = jnp.concatenate([flat0[local, :], flat1[local, :]], axis=1).astype(BF16)
            picked = jnp.dot(raw, fields, preferred_element_type=F32)
            even = even_ref[rows, :]
            even = jnp.concatenate([even, even], axis=1)
            for part, ref in ((0, x_re), (1, x_im)):
                both = picked[:, 256 * part : 256 * part + 256]
                evens = both * even
                ref[rows, :] = jnp.concatenate([evens, both - evens], axis=1).astype(BF16)

    light = pl.ds(0, LIGHT_COLS)
    heavy = pl.ds(LIGHT_COLS, COLS - LIGHT_COLS)

    wait_all(fl, 3, 2)
    unpack(recv_fl, LIGHT, 3, 2)
    build(0, LIGHT_COLS)

    @pl.loop(0, XROWS // XBLK)
    def _(b):
        rows = pl.ds(pl.multiple_of(b * XBLK, 16), XBLK)
        acc_c[rows, :] = jnp.dot(cos_xj[rows, light], x_re[light, :], preferred_element_type=F32)
        acc_s[rows, :] = jnp.dot(sin_xj[rows, light], x_im[light, :], preferred_element_type=F32)

    wait_all(fh, 2, 1)
    unpack(recv_fh, HEAVY, 2, 1)
    build(LIGHT_COLS, COLS - LIGHT_COLS)

    @pl.loop(0, XROWS // XBLK)
    def _(b):
        rows = pl.ds(pl.multiple_of(b * XBLK, 16), XBLK)
        c = acc_c[rows, :] + jnp.dot(
            cos_xj[rows, heavy], x_re[heavy, :], preferred_element_type=F32
        )
        s = acc_s[rows, :] + jnp.dot(
            sin_xj[rows, heavy], x_im[heavy, :], preferred_element_type=F32
        )
        c_sum, c_dif = c[:, :256] + c[:, 256:], c[:, :256] - c[:, 256:]
        s_sum, s_dif = s[:, :256] + s[:, 256:], s[:, :256] - s[:, 256:]

        def flux(g):
            return g[:, :128] * g[:, 128:]

        x = iota((XBLK, LANES), 0) + b * XBLK
        once = jnp.where((x == 0) | (x == LON // 4), 0.5, 1.0)
        f1 = flux(c_sum - s_sum) * once
        f2 = flux(c_sum + s_sum) * once
        f3 = flux(c_dif + s_dif) * once
        f4 = flux(c_dif - s_dif) * once
        near, far = f1 + f2, f3 + f4
        near_d, far_d = f2 - f1, f3 - f4
        h_c[rows, :] = jnp.concatenate([near + far, near - far], axis=1).astype(BF16)
        h_s[rows, :] = jnp.concatenate([near_d + far_d, near_d - far_d], axis=1).astype(BF16)

    places = place_fluxes()

    def direct(first_row, count):
        @pl.loop(0, count // LANES)
        def _(b):
            local = pl.ds(pl.multiple_of(b * LANES, LANES), LANES)
            rows = pl.ds(pl.multiple_of(first_row + b * LANES, LANES), LANES)
            c = jnp.dot(cos_jx[rows, :], h_c[...], preferred_element_type=F32)
            s = jnp.dot(sin_jx[rows, :], h_s[...], preferred_element_type=F32)
            even = even_ref[rows, :] > 0.5
            c = jnp.where(even, c[:, :128], c[:, 128:])
            s = jnp.where(even, s[:, :128], s[:, 128:])
            back = jnp.dot(
                jnp.concatenate([c, s], axis=1).astype(BF16), places, preferred_element_type=F32
            )
            flat0[local, :] = back[:, :LANES]
            flat1[local, :] = back[:, LANES:]

    def pack_back(send, rows, main, extra):
        @pl.loop(0, WAVES, unroll=8)
        def _(d):
            base = d * rows
            for q in range(main):
                send[d, q] = flat0[pl.ds(base + TILE * q, TILE), :].astype(BF16)

        @pl.when(core == 1)
        def _():
            @pl.loop(0, WAVES, unroll=8)
            def _(d):
                base = d * rows
                for q in range(extra):
                    first = flat1[pl.ds(base + TILE * q, TILE), :]
                    second = flat1[pl.ds(base + rows // 2 + TILE * q, TILE), :]
                    send[d, main + q] = jnp.where(lane4 < 64, first, second).astype(BF16)

    direct(LIGHT_COLS, COLS - LIGHT_COLS)
    pack_back(send_bh, HEAVY, 2, 1)
    send_all(bh, 2, 1)
    direct(0, LIGHT_COLS)
    pack_back(send_bl, LIGHT, 3, 2)
    send_all(bl, 3, 2)

    def unpack_back(recv, stage, rows, main, extra):
        @pl.loop(0, WAVES, unroll=8)
        def _(w):
            for q in range(main):
                stage[pl.ds(w * rows + TILE * q, TILE), :] = recv[w, q].astype(F32)

        @pl.when(core == 1)
        def _():
            @pl.loop(0, WAVES // 2, unroll=8)
            def _(e):
                base = (WAVES + e) * rows
                later = []
                for q in reversed(range(extra)):
                    low = recv[2 * e, main + q].astype(F32)
                    high = recv[2 * e + 1, main + q].astype(F32)
                    first = jnp.where(lane4 < 64, low, pltpu.roll(high, 64, 1))
                    second = jnp.where(lane4 < 64, pltpu.roll(low, 64, 1), high)
                    stage[pl.ds(base + TILE * q, TILE), :] = first
                    later.append((base + rows // 2 + TILE * q, second))
                for place, value in reversed(later):
                    stage[pl.ds(place, TILE), :] = value

    def e1_copy(g):
        window = (slice(None), pl.ds(2 * g, 2), slice(None), pl.ds(0, WIDTHS[g]))
        return pltpu.make_async_remote_copy(
            partial.at[(1 - core,) + window], e1_recv.at[window], e1_ss.at[g], e1_rs.at[g],
            device_id=(me, partner), device_id_type=MESH,
        )

    def row_piece(ref, g):
        return ref.at[pl.ds(2 * g, 2), :, pl.ds(0, WIDTHS[g])]

    def ends(g):
        near, far = lax.rem(y + 1, 4), lax.rem(y + 3, 4)
        return (near, up, far, down) if g in UP else (far, down, near, up)

    def rel_copy(g):
        return pltpu.make_async_remote_copy(
            piece(e2_send, lax.rem(y + 2, 4), g), row_piece(rel_recv, g), rel_ss.at[g], rel_rs.at[g],
            device_id=(me, ends(g)[1]), device_id_type=MESH,
        )

    def e2_copy(g):
        return pltpu.make_async_remote_copy(
            piece(e2_send, ends(g)[2], g), piece(e2_recv, 1, g), e2_ss.at[g], e2_rs.at[g],
            device_id=(me, ends(g)[3]), device_id_type=MESH,
        )

    def sum_copy(g):
        return pltpu.make_async_remote_copy(
            row_piece(e2_sum, g), piece(e2_recv, 0, g), sum_ss.at[g], sum_rs.at[g],
            device_id=(me, ends(g)[1]), device_id_type=MESH,
        )

    def add_cores(g):
        e1_copy(g).wait()
        for r in (2 * g, 2 * g + 1):
            for q in range(4):
                mine = partial[core, q, r, :, 0 : WIDTHS[g]].astype(F32)
                other = e1_recv[q, r, :, 0 : WIDTHS[g]].astype(F32)
                e2_send[q, r, :, 0 : WIDTHS[g]] = (mine + other).astype(BF16)
        rel_copy(g).start()
        e2_copy(g).start()

    def add_relayed(g):
        rel_copy(g).wait()
        for r in (2 * g, 2 * g + 1):
            mine = e2_send[ends(g)[0], r, :, 0 : WIDTHS[g]].astype(F32)
            other = rel_recv[r, :, 0 : WIDTHS[g]].astype(F32)
            e2_sum[r, :, 0 : WIDTHS[g]] = (mine + other).astype(BF16)
        sum_copy(g).start()

    def flux_rows(g):
        width = WIDTHS[g]
        for r in (2 * g, 2 * g + 1):
            table = table_rows(tabs, r, width)
            order = wo_ref[me * ROWS + r]
            weight = jnp.where(order == 0, 1.0, 0.5)
            factor = jnp.where(order < cut, area * weight, 0.0)
            if r < HEAVY:
                back = stage_h[pl.ds(r, LANES, stride=HEAVY), :]
            else:
                back = stage_l[pl.ds(r - HEAVY, LANES, stride=LIGHT), :]
            sums = lax.dot_general(
                (back.T * factor).astype(BF16), table, (((1,), (1,)), ((), ())),
                preferred_element_type=F32,
            )
            sums = sums.reshape(LEVS, 2, 8, width)
            sums = (sums[:, 0] + sums[:, 1] * sign[:, :width]).astype(BF16)
            for l in range(LEVS):
                partial[l % 2, l // 2, r, :, 0:width] = sums[l]
        e1_copy(g).start()

    wait_all(bh, 2, 1)
    unpack_back(recv_bh, stage_h, HEAVY, 2, 1)
    for g in range(GROUPS):
        if g == HEAVY // 2:
            add_cores(g - 1)
            add_relayed(g - 2)
            add_relayed(g - 1)
            wait_all(bl, 3, 2)
            unpack_back(recv_bl, stage_l, LIGHT, 3, 2)
        flux_rows(g)
        if g > 0 and g != HEAVY // 2:
            add_cores(g - 1)
        if g > 1 and g not in (HEAVY // 2, HEAVY // 2 + 1):
            add_relayed(g - 2)
    add_cores(GROUPS - 1)
    add_relayed(GROUPS - 2)
    add_relayed(GROUPS - 1)
    for g in range(GROUPS):
        width = WIDTHS[g]
        e2_copy(g).wait()
        sum_copy(g).wait()
        for r in (2 * g, 2 * g + 1):
            total = e2_send[y, r, :, 0:width].astype(F32) + e2_recv[0, r, :, 0:width].astype(F32)
            total = total + e2_recv[1, r, :, 0:width].astype(F32)
            out_ref[0, r, :, 0:width] = total.astype(BF16)
            if width < TOP:
                out_ref[0, r, :, width:TOP] = jnp.zeros((8, TOP - width), BF16)


def on_device(spectra, wave_order, truncation):
    by_peer = wave_order.reshape(WAVES, ROWS)
    orders = jnp.concatenate(
        [by_peer[:, HEAVY:].reshape(LIGHT_COLS), by_peer[:, :HEAVY].reshape(COLS - LIGHT_COLS), truncation]
    ).reshape(2 * COLS // LANES, LANES)
    vmem = pl.BlockSpec(memory_space=pltpu.VMEM)
    dma = pltpu.SemaphoreType.DMA
    message = lambda tiles: pltpu.VMEM((WAVES, tiles, TILE, LANES), BF16)
    flux = pl.pallas_call(
        kernel,
        out_shape=jax.ShapeDtypeStruct((1, ROWS, 8, TOP), BF16),
        in_specs=[pl.BlockSpec(memory_space=pltpu.SMEM), vmem, pl.BlockSpec(memory_space=pl.ANY)],
        out_specs=vmem,
        scratch_shapes=[
            pltpu.VMEM((10, ROWS_PAD, LANES), F32),
            pltpu.VMEM((10, ROWS_PAD, LANES), F32),
            pltpu.VMEM((8 * TAB_STRIDE[0], LANES), F32),
            pltpu.VMEM((8 * TAB_STRIDE[1], LANES), F32),
            pltpu.VMEM((8 * TAB_STRIDE[2], LANES), F32),
            pltpu.VMEM((XPAD, COLS), BF16),
            pltpu.VMEM((XPAD, COLS), BF16),
            pltpu.VMEM((COLS, XPAD), BF16),
            pltpu.VMEM((COLS, XPAD), BF16),
            pltpu.VMEM((COLS, LANES), F32),
            pltpu.VMEM((LEVS, ROWS, 8, TOP), BF16),
            pltpu.VMEM((LANES * LIGHT + 8, LANES), F32),
            pltpu.VMEM((LANES * HEAVY + 8, LANES), F32),
            message(5), message(3), message(5), message(3),
            message(5), message(3), message(5), message(3),
            pltpu.VMEM((LIGHT_COLS + 8, LANES), F32),
            pltpu.VMEM((LIGHT_COLS + 8, LANES), F32),
            pltpu.VMEM((COLS, 512), BF16),
            pltpu.VMEM((COLS, 512), BF16),
            pltpu.VMEM((XROWS, 512), F32),
            pltpu.VMEM((XROWS, 512), F32),
            pltpu.VMEM((XPAD, 256), BF16),
            pltpu.VMEM((XPAD, 256), BF16),
            pltpu.VMEM((2, 4, ROWS, 8, TOP), BF16),
            pltpu.VMEM((4, ROWS, 8, TOP), BF16),
            pltpu.VMEM((4, ROWS, 8, TOP), BF16),
            pltpu.VMEM((ROWS, 8, TOP), BF16),
            pltpu.VMEM((ROWS, 8, TOP), BF16),
            pltpu.VMEM((2, ROWS, 8, TOP), BF16),
            dma,
            dma((2, GROUPS)), dma((2, GROUPS)), dma((GROUPS,)), dma((GROUPS,)),
            dma((4, GROUPS)), dma((4, GROUPS)),
            dma, dma, dma, dma, dma, dma, dma, dma,
            dma((GROUPS,)), dma((GROUPS,)), dma((GROUPS,)), dma((GROUPS,)),
            dma((GROUPS,)), dma((GROUPS,)), dma((GROUPS,)), dma((GROUPS,)),
        ],
        compiler_params=pltpu.CompilerParams(
            collective_id=0, has_side_effects=True, vmem_limit_bytes=60 * 2**20
        ),
        name="flux_transform",
    )(wave_order, orders, spectra)
    return flux.astype(F32)


def solution(mesh):
    return jax.shard_map(
        on_device,
        mesh=mesh,
        in_specs=(P("lev", "wave", None, None), P(), P()),
        out_specs=P("lev", "wave", None, None),
        check_vma=False,
    )
```

```python
import functools
import math

import jax
import jax.numpy as jnp
from jax import lax
from jax.experimental import pallas as pl
from jax.experimental.pallas import tpu as pltpu
from jax.sharding import PartitionSpec as P

MESH = pl.DeviceIdType.MESH
F32 = jnp.float32
BF16 = jnp.bfloat16

TOP = 1280
LON = 2560
ROWS = 20
ROWS_PAD = 24
LIGHT = 12
HEAVY = 8
WAVES = 64
LEVS = 8
LANES = 128
RESCALE = 16
GROUPS = ROWS // 2
WIDTHS = tuple(TOP - LANES * g for g in range(GROUPS))
TAB_LEN = (1280, 768, 256)
TAB_STRIDE = (1288, 776, 264)
COLS = WAVES * ROWS
LIGHT_COLS = WAVES * LIGHT
XROWS = 672
XPAD = 768
XBLK = 112
TILE = 4


def iota(shape, dim):
    return lax.broadcasted_iota(jnp.int32, shape, dim)


def first_latitude(lev):
    return 160 * (lev // 2) + 64 * (lev % 2)


def half_angles(lat0):
    lat = iota((8, LANES), 1) + lat0
    return math.pi / TOP * (lat.astype(F32) + 0.5)


def own_orders(wo_ref, base):
    rows = iota((ROWS_PAD, LANES), 0)
    orders = jnp.full((ROWS_PAD, LANES), TOP, jnp.int32)
    for r in range(ROWS):
        orders = jnp.where(rows == r, wo_ref[base + r], orders)
    return orders


def recurrence_start(wo_ref, base, orders, lat0, alpha_ref, both_ref):
    place = iota((16, LANES), 0) * LANES + iota((16, LANES), 1)
    j = jnp.maximum(place, 1).astype(F32)
    terms = jnp.where((place >= 1) & (place < TOP), jnp.log((2.0 * j + 1.0) / (2.0 * j)), 0.0)
    rows = iota((ROWS_PAD, LANES), 0)
    logs = jnp.zeros((ROWS_PAD, LANES), F32)
    for r in range(ROWS):
        part = jnp.where(place <= wo_ref[base + r], terms, 0.0)
        total = jnp.sum(jnp.sum(part, axis=0, keepdims=True), axis=1, keepdims=True)
        logs = jnp.where(rows == r, total, logs)
    order = orders.astype(F32)
    angles = half_angles(lat0)
    cosine = jnp.cos(angles)
    log_sine = jnp.log(jnp.sin(angles))
    for kb in range(TOP // LANES):
        k = iota((ROWS_PAD, LANES), 1) + (kb * LANES + 1)
        kf = k.astype(F32)
        n = order + kf
        alpha = jnp.sqrt((4.0 * n * n - 1.0) / (kf * (n + order)))
        low = n - 1.0
        beta = jnp.sqrt(
            (kf - 1.0) * (kf - 1.0 + 2.0 * order) / jnp.maximum(4.0 * low * low - 1.0, 1.0)
        )
        kept = orders + k < TOP
        alpha_ref[kb] = jnp.where(kept, alpha, 0.0)
        both_ref[kb] = jnp.where(kept, alpha * beta, 0.0)
    state = []
    for g in range(3):
        part = slice(8 * g, 8 * g + 8)
        scale = 0.5 * math.log(0.5) + 0.5 * logs[part] + order[part] * log_sine
        state += [jnp.zeros((8, LANES), F32), jnp.ones((8, LANES), F32), scale]
    return cosine, state


def recurrence_phase(phase, cosine, state, alpha_ref, both_ref, tabs):
    live, start, stop = ((3, 0, 2), (2, 2, 6), (1, 6, 10))[phase]

    def block(kb, flat):
        st = [tuple(flat[3 * g : 3 * g + 3]) for g in range(live)]
        alpha = alpha_ref[kb]
        both = both_ref[kb]
        for i in range(LANES):
            if i % RESCALE == 0:
                factor = [jnp.exp(s[2]) for s in st]
            for g in range(live):
                prev, cur, scale = st[g]
                rows = pl.ds(kb * LANES + i, 8, stride=TAB_STRIDE[g])
                tabs[g][rows, :] = cur * factor[g]
                part = slice(8 * g, 8 * g + 8)
                fresh = (alpha[part, i : i + 1] * cosine) * cur - both[part, i : i + 1] * prev
                st[g] = (cur, fresh, scale)
            if i % RESCALE == RESCALE - 1:
                for g in range(live):
                    prev, cur, scale = st[g]
                    big = jnp.maximum(jnp.maximum(jnp.abs(prev), jnp.abs(cur)), 1e-30)
                    inv = 1.0 / big
                    st[g] = (prev * inv, cur * inv, scale + jnp.log(big))
        return tuple(v for s in st for v in s)

    return list(lax.fori_loop(start, stop, block, tuple(state[: 3 * live])))


def table_rows(tabs, r, width):
    g = r // 8
    return tabs[g][pl.ds((r % 8) * TAB_STRIDE[g], width), :].astype(BF16)


def sin_cos(phase):
    turns = jnp.floor(phase * (1.0 / LON))
    phase = phase - turns * LON
    quarter = jnp.floor(phase * (4.0 / LON) + 0.5)
    t = (phase - quarter * (LON // 4)) * (2.0 * math.pi / LON)
    t2 = t * t
    s = t * (1.0 + t2 * (-1.0 / 6 + t2 * (1.0 / 120 + t2 * (-1.0 / 5040 + t2 * (1.0 / 362880)))))
    c = 1.0 + t2 * (-0.5 + t2 * (1.0 / 24 + t2 * (-1.0 / 720 + t2 * (1.0 / 40320))))
    odd = (quarter == 1.0) | (quarter == 3.0)
    sine = jnp.where(odd, c, s)
    cosine = jnp.where(odd, s, c)
    sine = jnp.where((quarter == 2.0) | (quarter == 3.0), -sine, sine)
    cosine = jnp.where((quarter == 1.0) | (quarter == 2.0), -cosine, cosine)
    return sine, cosine


def longitude_tables(mt_ref, cos_xj, sin_xj, cos_jx, sin_jx, even_ref):
    @pl.loop(0, COLS // LANES)
    def _(jb):
        cols = pl.ds(pl.multiple_of(jb * LANES, LANES), LANES)
        mj = mt_ref[pl.ds(jb, 1), :]
        mf = mj.astype(F32)
        sb, cb = sin_cos(mf * iota((32, LANES), 0).astype(F32))
        sa, ca = sin_cos(mf * (32 * iota((24, LANES), 0)).astype(F32))
        for xa in range(XPAD // 32):
            rows = pl.ds(32 * xa, 32)
            if xa > 20:
                cos_xj[rows, cols] = jnp.zeros((32, LANES), BF16)
                sin_xj[rows, cols] = jnp.zeros((32, LANES), BF16)
                continue
            sa1, ca1 = sa[xa : xa + 1], ca[xa : xa + 1]
            c = ca1 * cb - sa1 * sb
            s = sa1 * cb + ca1 * sb
            if xa == 20:
                c = jnp.where(iota((32, LANES), 0) == 0, c, 0.0)
                s = jnp.where(iota((32, LANES), 0) == 0, s, 0.0)
            cos_xj[rows, cols] = c.astype(BF16)
            sin_xj[rows, cols] = s.astype(BF16)
        even = jnp.where(lax.rem(mj, 2) == 0, 1.0, 0.0)
        even_ref[cols, :] = jnp.broadcast_to(even, (LANES, LANES)).T
        for xb in range(XPAD // LANES):
            rows = pl.ds(xb * LANES, LANES)
            cos_jx[cols, rows] = cos_xj[rows, cols].T
            sin_jx[cols, rows] = sin_xj[rows, cols].T


def grid_lane(u):
    slot, v = u // 64, u % 64
    flux = jnp.where(slot == 0, v // 16, v // 8)
    s = jnp.where(slot == 0, v // 8 % 2, v // 4 % 2)
    level = jnp.where(slot == 0, v % 8, v % 4)
    return slot, flux, s, level, (slot == 0) | (v < 32)


def pick_fields():
    row, col = iota((256, 512), 0), iota((256, 512), 1)
    slot, level, s, part, field = row // 128, row // 16 % 8, row // 8 % 2, row // 4 % 2, row % 4
    c_part, side = col // 256, col // 128 % 2
    c_slot, flux, c_s, c_level, used = grid_lane(col % 128)
    wanted = jnp.where(side == 0, flux % 2, 2 + flux // 2)
    same = used & (slot == c_slot) & (s == c_s) & (level == c_level)
    same = same & (part == c_part) & (field == wanted)
    return jnp.where(same, 1.0, 0.0).astype(BF16)


def place_fluxes():
    row, col = iota((256, 256), 0), iota((256, 256), 1)
    part = row // 128
    slot, flux, s, level, used = grid_lane(row % 128)
    c_slot = col // 128
    c_level = jnp.where(c_slot == 0, col // 16 % 8, col // 16 % 4)
    same = used & (slot == c_slot) & (level == c_level) & (s == col // 8 % 2)
    same = same & (part == col // 4 % 2) & (flux == col % 4)
    return jnp.where(same, 1.0, 0.0).astype(BF16)


def kernel(
    wo_ref, mt_ref, spec_ref, out_ref,
    alpha_ref, both_ref, tab0, tab1, tab2,
    cos_xj, sin_xj, cos_jx, sin_jx, even_ref,
    gath, stage_l, stage_h, send_fl, send_fh, recv_fl, recv_fh, send_bl, send_bh, recv_bl, recv_bh,
    flat0, flat1, x_re, x_im, acc_c, acc_s, h_c, h_s,
    partial, e1_recv, e2_send, e2_recv,
    z_ready, own_sem, g_send, g_recv, c_send, c_recv,
    fl_ss, fl_rs, fh_ss, fh_rs, bl_ss, bl_rs, bh_ss, bh_rs,
    e1_ss, e1_rs, e2_ss, e2_rs,
):
    me = lax.axis_index("wave")
    lev = lax.axis_index("lev")
    y = lev // 2
    core = lev % 2
    partner = y * 2 + (1 - core)
    x = lax.rem(me, 4)
    tabs = (tab0, tab1, tab2)
    lane4 = iota((TILE, LANES), 1)

    barrier = pltpu.get_barrier_semaphore()
    for i in range(1, 4):
        pl.semaphore_signal(
            barrier, inc=1, device_id=(me, lax.rem(lev + 2 * i, LEVS)), device_id_type=MESH
        )
    pl.semaphore_signal(barrier, inc=1, device_id=(me, partner), device_id_type=MESH)

    def x_peer(i):
        return me - x + lax.rem(x + i, 4)

    for i in range(1, 4):
        pl.semaphore_signal(barrier, inc=1, device_id=(x_peer(i), lev), device_id_type=MESH)
    for i in range(1, WAVES // 4):
        pl.semaphore_signal(
            barrier, inc=1, device_id=(lax.rem(me + 4 * i, WAVES), lev), device_id_type=MESH
        )

    lat0 = first_latitude(lev)
    orders = own_orders(wo_ref, me * ROWS)
    cosine, state = recurrence_start(wo_ref, me * ROWS, orders, lat0, alpha_ref, both_ref)
    flat0[...] = jnp.zeros_like(flat0)
    flat1[...] = jnp.zeros_like(flat1)
    h_c[pl.ds(XROWS, XPAD - XROWS), :] = jnp.zeros((XPAD - XROWS, 256), BF16)
    h_s[pl.ds(XROWS, XPAD - XROWS), :] = jnp.zeros((XPAD - XROWS, 256), BF16)

    pl.semaphore_wait(barrier, 3 + 1 + 3 + WAVES // 4 - 1)
    for i in range(1, 4):
        pl.semaphore_signal(z_ready, inc=1, device_id=(x_peer(i), lev), device_id_type=MESH)

    light_groups = tuple(range(HEAVY // 2, GROUPS))
    heavy_groups = tuple(range(HEAVY // 2))

    def piece(ref, level, g):
        return ref.at[level, pl.ds(2 * g, 2), :, pl.ds(0, WIDTHS[g])]

    def own_copy():
        return pltpu.make_async_copy(spec_ref.at[0], gath.at[lev], own_sem)

    def y_copy(i, g):
        return pltpu.make_async_remote_copy(
            piece(spec_ref, 0, g), piece(gath, lev, g), g_send.at[i, g], g_recv.at[i, g],
            device_id=(me, lax.rem(lev + 2 * i, LEVS)), device_id_type=MESH,
        )

    def core_copy(i, g):
        level = lax.rem(lev + LEVS - 2 * i, LEVS)
        src = piece(spec_ref, 0, g) if i == 0 else piece(gath, level, g)
        return pltpu.make_async_remote_copy(
            src, piece(gath, level, g), c_send.at[i, g], c_recv.at[i, g],
            device_id=(me, partner), device_id_type=MESH,
        )

    def pass_on(groups):
        for g in groups:
            for i in range(1, 4):
                y_copy(i, g).wait()
                core_copy(i, g).start()

    def gathered(groups):
        for g in groups:
            for i in range(4):
                core_copy(i, g).wait()

    for groups in (light_groups, heavy_groups):
        for g in groups:
            for i in range(1, 4):
                y_copy(i, g).start()
        for g in groups:
            core_copy(0, g).start()
    own_copy().start()

    angles = half_angles(lat0)[0:1]
    unit = lat0 // 32
    cut_row = COLS // LANES + unit // 4
    wide = jnp.concatenate([mt_ref[pl.ds(cut_row, 1), :], mt_ref[pl.ds(cut_row + 1, 1), :]], axis=1)
    cut = wide[:, 0:LANES]
    for n in range(1, 4):
        cut = jnp.where(unit % 4 == n, wide[:, 32 * n : 32 * n + LANES], cut)
    area = (float(TOP) / LON) * (math.pi / TOP) * jnp.sin(angles)
    area = jnp.where(iota((1, LANES), 1) < 64 + 32 * core, area, 0.0)
    sign = jnp.where(iota((1, TOP), 1) % 2 == 0, 1.0, -1.0)

    def legendre_row(r):
        width = WIDTHS[r // 2]
        table = table_rows(tabs, r, width)
        coeff = gath[:, r, :, 0:width].astype(F32)
        both_signs = jnp.stack([coeff, coeff * sign[:, :width]], axis=1).reshape(LANES, width)
        fourier = jnp.dot(both_signs.astype(BF16), table, preferred_element_type=F32)
        order = wo_ref[me * ROWS + r]
        weight = jnp.where(order == 0, 1.0, 2.0)
        fourier = fourier * jnp.where(order < cut, weight, 0.0)
        if r < HEAVY:
            stage_h[pl.ds(r, LANES, stride=HEAVY), :] = fourier.T
        else:
            stage_l[pl.ds(r - HEAVY, LANES, stride=LIGHT), :] = fourier.T

    def both_cores(main, extra, act):
        @pl.when(core == 0)
        def _():
            act(main)

        @pl.when(core == 1)
        def _():
            act(main + extra)

    def peer_copy(send, recv, ss, rs, i, count):
        to = lax.rem(me + i, WAVES)
        return pltpu.make_async_remote_copy(
            send.at[to, pl.ds(0, count)], recv.at[me, pl.ds(0, count)], ss, rs,
            device_id=(to, lev), device_id_type=MESH,
        )

    def send_all(bufs, main, extra):
        def start(count):
            @pl.loop(1, WAVES, unroll=7)
            def _(i):
                peer_copy(*bufs, i, count).start()

        both_cores(main, extra, start)
        bufs[1][me] = bufs[0][me]

    def wait_all(bufs, main, extra):
        send, recv, ss, rs = bufs

        def wait(count):
            window = (pl.ds(0, WAVES - 1), pl.ds(0, count))
            pltpu.make_async_copy(send.at[window], send.at[window], ss).wait()
            pltpu.make_async_copy(recv.at[window], recv.at[window], rs).wait()

        both_cores(main, extra, wait)

    fl = (send_fl, recv_fl, fl_ss, fl_rs)
    fh = (send_fh, recv_fh, fh_ss, fh_rs)
    bl = (send_bl, recv_bl, bl_ss, bl_rs)
    bh = (send_bh, recv_bh, bh_ss, bh_rs)

    def pack(stage, send, rows, main, extra):
        @pl.loop(0, WAVES, unroll=8)
        def _(w):
            for q in range(main):
                send[w, q] = stage[pl.ds(w * rows + TILE * q, TILE), :].astype(BF16)

        @pl.when(core == 1)
        def _():
            @pl.loop(0, WAVES // 2, unroll=8)
            def _(e):
                base = (WAVES + e) * rows
                for q in range(extra):
                    first = stage[pl.ds(base + TILE * q, TILE), :]
                    second = stage[pl.ds(base + rows // 2 + TILE * q, TILE), :]
                    second = pltpu.roll(second, 64, 1)
                    send[2 * e, main + q] = jnp.where(lane4 < 64, first, second).astype(BF16)
                    send[2 * e + 1, main + q] = jnp.where(lane4 < 64, second, first).astype(BF16)

    state = recurrence_phase(0, cosine, state, alpha_ref, both_ref, tabs)
    state = recurrence_phase(1, cosine, state, alpha_ref, both_ref, tabs)
    pass_on(light_groups)
    recurrence_phase(2, cosine, state, alpha_ref, both_ref, tabs)
    own_copy().wait()
    gathered(light_groups)
    for r in range(HEAVY, ROWS):
        legendre_row(r)
    pack(stage_l, send_fl, LIGHT, 3, 2)
    pl.semaphore_wait(z_ready, 3)
    send_all(fl, 3, 2)

    pass_on(heavy_groups)
    gathered(heavy_groups)
    for r in range(HEAVY):
        legendre_row(r)
    pack(stage_h, send_fh, HEAVY, 2, 1)
    send_all(fh, 2, 1)

    longitude_tables(mt_ref, cos_xj, sin_xj, cos_jx, sin_jx, even_ref)

    fields = pick_fields()

    def unpack(recv, rows, main, extra):
        @pl.loop(0, WAVES, unroll=8)
        def _(d):
            base = d * rows
            for q in range(main):
                flat0[pl.ds(base + TILE * q, TILE), :] = recv[d, q].astype(F32)

        @pl.when(core == 1)
        def _():
            odd = me % 2 == 1

            @pl.loop(0, WAVES, unroll=8)
            def _(d):
                base = d * rows
                later = []
                for q in reversed(range(extra)):
                    here = recv[d, main + q].astype(F32)
                    there = pltpu.roll(here, 64, 1)
                    flat1[pl.ds(base + TILE * q, TILE), :] = jnp.where(odd, there, here)
                    later.append((base + rows // 2 + TILE * q, jnp.where(odd, here, there)))
                for place, value in reversed(later):
                    flat1[pl.ds(place, TILE), :] = value

    def build(first_row, count):
        @pl.loop(0, count // LANES)
        def _(b):
            local = pl.ds(pl.multiple_of(b * LANES, LANES), LANES)
            rows = pl.ds(pl.multiple_of(first_row + b * LANES, LANES), LANES)
            raw = jnp.concatenate([flat0[local, :], flat1[local, :]], axis=1).astype(BF16)
            picked = jnp.dot(raw, fields, preferred_element_type=F32)
            even = even_ref[rows, :]
            even = jnp.concatenate([even, even], axis=1)
            for part, ref in ((0, x_re), (1, x_im)):
                both = picked[:, 256 * part : 256 * part + 256]
                evens = both * even
                ref[rows, :] = jnp.concatenate([evens, both - evens], axis=1).astype(BF16)

    light = pl.ds(0, LIGHT_COLS)
    heavy = pl.ds(LIGHT_COLS, COLS - LIGHT_COLS)

    wait_all(fl, 3, 2)
    unpack(recv_fl, LIGHT, 3, 2)
    build(0, LIGHT_COLS)

    @pl.loop(0, XROWS // XBLK)
    def _(b):
        rows = pl.ds(pl.multiple_of(b * XBLK, 16), XBLK)
        acc_c[rows, :] = jnp.dot(cos_xj[rows, light], x_re[light, :], preferred_element_type=F32)
        acc_s[rows, :] = jnp.dot(sin_xj[rows, light], x_im[light, :], preferred_element_type=F32)

    wait_all(fh, 2, 1)
    unpack(recv_fh, HEAVY, 2, 1)
    build(LIGHT_COLS, COLS - LIGHT_COLS)

    @pl.loop(0, XROWS // XBLK)
    def _(b):
        rows = pl.ds(pl.multiple_of(b * XBLK, 16), XBLK)
        c = acc_c[rows, :] + jnp.dot(
            cos_xj[rows, heavy], x_re[heavy, :], preferred_element_type=F32
        )
        s = acc_s[rows, :] + jnp.dot(
            sin_xj[rows, heavy], x_im[heavy, :], preferred_element_type=F32
        )
        c_sum, c_dif = c[:, :256] + c[:, 256:], c[:, :256] - c[:, 256:]
        s_sum, s_dif = s[:, :256] + s[:, 256:], s[:, :256] - s[:, 256:]

        def flux(g):
            return g[:, :128] * g[:, 128:]

        place = iota((XBLK, LANES), 0) + b * XBLK
        once = jnp.where((place == 0) | (place == LON // 4), 0.5, 1.0)
        f1 = flux(c_sum - s_sum) * once
        f2 = flux(c_sum + s_sum) * once
        f3 = flux(c_dif + s_dif) * once
        f4 = flux(c_dif - s_dif) * once
        near, far = f1 + f2, f3 + f4
        near_d, far_d = f2 - f1, f3 - f4
        h_c[rows, :] = jnp.concatenate([near + far, near - far], axis=1).astype(BF16)
        h_s[rows, :] = jnp.concatenate([near_d + far_d, near_d - far_d], axis=1).astype(BF16)

    places = place_fluxes()

    def direct(first_row, count):
        @pl.loop(0, count // LANES)
        def _(b):
            local = pl.ds(pl.multiple_of(b * LANES, LANES), LANES)
            rows = pl.ds(pl.multiple_of(first_row + b * LANES, LANES), LANES)
            c = jnp.dot(cos_jx[rows, :], h_c[...], preferred_element_type=F32)
            s = jnp.dot(sin_jx[rows, :], h_s[...], preferred_element_type=F32)
            even = even_ref[rows, :] > 0.5
            c = jnp.where(even, c[:, :128], c[:, 128:])
            s = jnp.where(even, s[:, :128], s[:, 128:])
            back = jnp.dot(
                jnp.concatenate([c, s], axis=1).astype(BF16), places, preferred_element_type=F32
            )
            flat0[local, :] = back[:, :LANES]
            flat1[local, :] = back[:, LANES:]

    def pack_back(send, rows, main, extra):
        @pl.loop(0, WAVES, unroll=8)
        def _(d):
            base = d * rows
            for q in range(main):
                send[d, q] = flat0[pl.ds(base + TILE * q, TILE), :].astype(BF16)

        @pl.when(core == 1)
        def _():
            @pl.loop(0, WAVES, unroll=8)
            def _(d):
                base = d * rows
                for q in range(extra):
                    first = flat1[pl.ds(base + TILE * q, TILE), :]
                    second = flat1[pl.ds(base + rows // 2 + TILE * q, TILE), :]
                    send[d, main + q] = jnp.where(lane4 < 64, first, second).astype(BF16)

    direct(LIGHT_COLS, COLS - LIGHT_COLS)
    pack_back(send_bh, HEAVY, 2, 1)
    send_all(bh, 2, 1)
    direct(0, LIGHT_COLS)
    pack_back(send_bl, LIGHT, 3, 2)
    send_all(bl, 3, 2)

    def unpack_back(recv, stage, rows, main, extra):
        @pl.loop(0, WAVES, unroll=8)
        def _(w):
            for q in range(main):
                stage[pl.ds(w * rows + TILE * q, TILE), :] = recv[w, q].astype(F32)

        @pl.when(core == 1)
        def _():
            @pl.loop(0, WAVES // 2, unroll=8)
            def _(e):
                base = (WAVES + e) * rows
                later = []
                for q in reversed(range(extra)):
                    low = recv[2 * e, main + q].astype(F32)
                    high = recv[2 * e + 1, main + q].astype(F32)
                    first = jnp.where(lane4 < 64, low, pltpu.roll(high, 64, 1))
                    second = jnp.where(lane4 < 64, pltpu.roll(low, 64, 1), high)
                    stage[pl.ds(base + TILE * q, TILE), :] = first
                    later.append((base + rows // 2 + TILE * q, second))
                for place, value in reversed(later):
                    stage[pl.ds(place, TILE), :] = value

    def e1_copy(g):
        window = (slice(None), pl.ds(2 * g, 2), slice(None), pl.ds(0, WIDTHS[g]))
        return pltpu.make_async_remote_copy(
            partial.at[(1 - core,) + window], e1_recv.at[window], e1_ss.at[g], e1_rs.at[g],
            device_id=(me, partner), device_id_type=MESH,
        )

    def e2_copy(i, g):
        to = lax.rem(y + i, 4)
        return pltpu.make_async_remote_copy(
            piece(e2_send, to, g), piece(e2_recv, i - 1, g), e2_ss.at[i, g], e2_rs.at[i, g],
            device_id=(me, to * 2 + core), device_id_type=MESH,
        )

    def add_cores(g):
        e1_copy(g).wait()
        for r in (2 * g, 2 * g + 1):
            for q in range(4):
                mine = partial[core, q, r, :, 0 : WIDTHS[g]].astype(F32)
                other = e1_recv[q, r, :, 0 : WIDTHS[g]].astype(F32)
                e2_send[q, r, :, 0 : WIDTHS[g]] = (mine + other).astype(BF16)
        for i in (2, 1, 3):
            e2_copy(i, g).start()

    def flux_rows(g):
        width = WIDTHS[g]
        for r in (2 * g, 2 * g + 1):
            table = table_rows(tabs, r, width)
            order = wo_ref[me * ROWS + r]
            weight = jnp.where(order == 0, 1.0, 0.5)
            factor = jnp.where(order < cut, area * weight, 0.0)
            if r < HEAVY:
                back = stage_h[pl.ds(r, LANES, stride=HEAVY), :]
            else:
                back = stage_l[pl.ds(r - HEAVY, LANES, stride=LIGHT), :]
            sums = lax.dot_general(
                (back.T * factor).astype(BF16), table, (((1,), (1,)), ((), ())),
                preferred_element_type=F32,
            )
            sums = sums.reshape(LEVS, 2, 8, width)
            sums = (sums[:, 0] + sums[:, 1] * sign[:, :width]).astype(BF16)
            for l in range(LEVS):
                partial[l % 2, l // 2, r, :, 0:width] = sums[l]
        e1_copy(g).start()

    wait_all(bh, 2, 1)
    unpack_back(recv_bh, stage_h, HEAVY, 2, 1)
    for g in heavy_groups:
        flux_rows(g)
    for g in heavy_groups:
        add_cores(g)
    wait_all(bl, 3, 2)
    unpack_back(recv_bl, stage_l, LIGHT, 3, 2)
    for g in light_groups:
        flux_rows(g)
    for g in light_groups:
        add_cores(g)
    for g in range(GROUPS):
        width = WIDTHS[g]
        for i in range(1, 4):
            e2_copy(i, g).wait()
        for r in (2 * g, 2 * g + 1):
            total = e2_send[y, r, :, 0:width].astype(F32)
            for i in range(3):
                total = total + e2_recv[i, r, :, 0:width].astype(F32)
            out_ref[0, r, :, 0:width] = total.astype(BF16)
            if width < TOP:
                out_ref[0, r, :, width:TOP] = jnp.zeros((8, TOP - width), BF16)


def on_device(spectra, wave_order, truncation):
    by_peer = wave_order.reshape(WAVES, ROWS)
    orders = jnp.concatenate(
        [by_peer[:, HEAVY:].reshape(LIGHT_COLS), by_peer[:, :HEAVY].reshape(COLS - LIGHT_COLS), truncation]
    ).reshape(2 * COLS // LANES, LANES)
    vmem = pl.BlockSpec(memory_space=pltpu.VMEM)
    dma = pltpu.SemaphoreType.DMA
    message = lambda tiles: pltpu.VMEM((WAVES, tiles, TILE, LANES), BF16)
    flux = pl.pallas_call(
        kernel,
        out_shape=jax.ShapeDtypeStruct((1, ROWS, 8, TOP), BF16),
        in_specs=[pl.BlockSpec(memory_space=pltpu.SMEM), vmem, pl.BlockSpec(memory_space=pl.ANY)],
        out_specs=vmem,
        scratch_shapes=[
            pltpu.VMEM((10, ROWS_PAD, LANES), F32),
            pltpu.VMEM((10, ROWS_PAD, LANES), F32),
            pltpu.VMEM((8 * TAB_STRIDE[0], LANES), F32),
            pltpu.VMEM((8 * TAB_STRIDE[1], LANES), F32),
            pltpu.VMEM((8 * TAB_STRIDE[2], LANES), F32),
            pltpu.VMEM((XPAD, COLS), BF16),
            pltpu.VMEM((XPAD, COLS), BF16),
            pltpu.VMEM((COLS, XPAD), BF16),
            pltpu.VMEM((COLS, XPAD), BF16),
            pltpu.VMEM((COLS, LANES), F32),
            pltpu.VMEM((LEVS, ROWS, 8, TOP), BF16),
            pltpu.VMEM((LANES * LIGHT + 8, LANES), F32),
            pltpu.VMEM((LANES * HEAVY + 8, LANES), F32),
            message(5), message(3), message(5), message(3),
            message(5), message(3), message(5), message(3),
            pltpu.VMEM((LIGHT_COLS + 8, LANES), F32),
            pltpu.VMEM((LIGHT_COLS + 8, LANES), F32),
            pltpu.VMEM((COLS, 512), BF16),
            pltpu.VMEM((COLS, 512), BF16),
            pltpu.VMEM((XROWS, 512), F32),
            pltpu.VMEM((XROWS, 512), F32),
            pltpu.VMEM((XPAD, 256), BF16),
            pltpu.VMEM((XPAD, 256), BF16),
            pltpu.VMEM((2, 4, ROWS, 8, TOP), BF16),
            pltpu.VMEM((4, ROWS, 8, TOP), BF16),
            pltpu.VMEM((4, ROWS, 8, TOP), BF16),
            pltpu.VMEM((3, ROWS, 8, TOP), BF16),
            pltpu.SemaphoreType.REGULAR,
            dma,
            dma((4, GROUPS)), dma((4, GROUPS)), dma((4, GROUPS)), dma((4, GROUPS)),
            dma, dma, dma, dma, dma, dma, dma, dma,
            dma((GROUPS,)), dma((GROUPS,)), dma((4, GROUPS)), dma((4, GROUPS)),
        ],
        compiler_params=pltpu.CompilerParams(
            collective_id=0, has_side_effects=True, vmem_limit_bytes=60 * 2**20
        ),
        name="flux_transform",
    )(wave_order, orders, spectra)
    return flux.astype(F32)


def solution(mesh):
    return jax.shard_map(
        on_device,
        mesh=mesh,
        in_specs=(P("lev", "wave", None, None), P(), P()),
        out_specs=P("lev", "wave", None, None),
        check_vma=False,
    )
```

```python
import functools
import math

import jax
import jax.numpy as jnp
from jax import lax
from jax.experimental import pallas as pl
from jax.experimental.pallas import tpu as pltpu
from jax.sharding import PartitionSpec as P

MESH = pl.DeviceIdType.MESH
F32 = jnp.float32
BF16 = jnp.bfloat16

TOP = 1280
LON = 2560
ROWS = 20
ROWS_PAD = 24
HEAVY = 8
WAVES = 64
LEVS = 8
LANES = 128
RESCALE = 16
GROUPS = ROWS // 2
WIDTHS = tuple(TOP - LANES * g for g in range(GROUPS))
TAB_LEN = (1280, 768, 256)
TAB_STRIDE = (1288, 776, 264)
COLS = WAVES * ROWS
HEAVY_COLS = WAVES * HEAVY
XROWS = 672
XPAD = 768
XBLK = 224
TILE = 4
HEAVY_TILES = (0, 1)
LIGHT_TILES = (2, 3, 4)
HEAVY_PAIRS = ((0, 1),)
LIGHT_PAIRS = ((2, 3), (4, 4))
HALF = WAVES // 2


def iota(shape, dim):
    return lax.broadcasted_iota(jnp.int32, shape, dim)


def first_latitude(lev):
    return 160 * (lev // 2) + 64 * (lev % 2)


def half_angles(lat0):
    lat = iota((8, LANES), 1) + lat0
    return math.pi / TOP * (lat.astype(F32) + 0.5)


def own_orders(wo_ref, base):
    rows = iota((ROWS_PAD, LANES), 0)
    orders = jnp.full((ROWS_PAD, LANES), TOP, jnp.int32)
    for r in range(ROWS):
        orders = jnp.where(rows == r, wo_ref[base + r], orders)
    return orders


def recurrence_start(wo_ref, base, orders, lat0, alpha_ref, both_ref):
    place = iota((16, LANES), 0) * LANES + iota((16, LANES), 1)
    j = jnp.maximum(place, 1).astype(F32)
    terms = jnp.where((place >= 1) & (place < TOP), jnp.log((2.0 * j + 1.0) / (2.0 * j)), 0.0)
    rows = iota((ROWS_PAD, LANES), 0)
    logs = jnp.zeros((ROWS_PAD, LANES), F32)
    for r in range(ROWS):
        part = jnp.where(place <= wo_ref[base + r], terms, 0.0)
        total = jnp.sum(jnp.sum(part, axis=0, keepdims=True), axis=1, keepdims=True)
        logs = jnp.where(rows == r, total, logs)
    order = orders.astype(F32)
    angles = half_angles(lat0)
    cosine = jnp.cos(angles)
    log_sine = jnp.log(jnp.sin(angles))
    for kb in range(TOP // LANES):
        k = iota((ROWS_PAD, LANES), 1) + (kb * LANES + 1)
        kf = k.astype(F32)
        n = order + kf
        alpha = jnp.sqrt((4.0 * n * n - 1.0) / (kf * (n + order)))
        low = n - 1.0
        beta = jnp.sqrt(
            (kf - 1.0) * (kf - 1.0 + 2.0 * order) / jnp.maximum(4.0 * low * low - 1.0, 1.0)
        )
        kept = orders + k < TOP
        alpha_ref[kb] = jnp.where(kept, alpha, 0.0)
        both_ref[kb] = jnp.where(kept, alpha * beta, 0.0)
    state = []
    for g in range(3):
        part = slice(8 * g, 8 * g + 8)
        scale = 0.5 * math.log(0.5) + 0.5 * logs[part] + order[part] * log_sine
        state += [jnp.zeros((8, LANES), F32), jnp.ones((8, LANES), F32), scale]
    return cosine, state


def recurrence_phase(phase, cosine, state, alpha_ref, both_ref, tabs):
    live, start, stop = ((3, 0, 2), (2, 2, 6), (1, 6, 10))[phase]

    def block(kb, flat):
        st = [tuple(flat[3 * g : 3 * g + 3]) for g in range(live)]
        alpha = alpha_ref[kb]
        both = both_ref[kb]
        for i in range(LANES):
            if i % RESCALE == 0:
                factor = [jnp.exp(s[2]) for s in st]
            for g in range(live):
                prev, cur, scale = st[g]
                rows = pl.ds(kb * LANES + i, 8, stride=TAB_STRIDE[g])
                tabs[g][rows, :] = cur * factor[g]
                part = slice(8 * g, 8 * g + 8)
                fresh = (alpha[part, i : i + 1] * cosine) * cur - both[part, i : i + 1] * prev
                st[g] = (cur, fresh, scale)
            if i % RESCALE == RESCALE - 1:
                for g in range(live):
                    prev, cur, scale = st[g]
                    big = jnp.maximum(jnp.maximum(jnp.abs(prev), jnp.abs(cur)), 1e-30)
                    inv = 1.0 / big
                    st[g] = (prev * inv, cur * inv, scale + jnp.log(big))
        return tuple(v for s in st for v in s)

    return list(lax.fori_loop(start, stop, block, tuple(state[: 3 * live])))


def table_rows(tabs, r, width):
    g = r // 8
    return tabs[g][pl.ds((r % 8) * TAB_STRIDE[g], width), :].astype(BF16)


def sin_cos(phase):
    turns = jnp.floor(phase * (1.0 / LON))
    phase = phase - turns * LON
    quarter = jnp.floor(phase * (4.0 / LON) + 0.5)
    t = (phase - quarter * (LON // 4)) * (2.0 * math.pi / LON)
    t2 = t * t
    s = t * (1.0 + t2 * (-1.0 / 6 + t2 * (1.0 / 120 + t2 * (-1.0 / 5040 + t2 * (1.0 / 362880)))))
    c = 1.0 + t2 * (-0.5 + t2 * (1.0 / 24 + t2 * (-1.0 / 720 + t2 * (1.0 / 40320))))
    odd = (quarter == 1.0) | (quarter == 3.0)
    sine = jnp.where(odd, c, s)
    cosine = jnp.where(odd, s, c)
    sine = jnp.where((quarter == 2.0) | (quarter == 3.0), -sine, sine)
    cosine = jnp.where((quarter == 1.0) | (quarter == 2.0), -cosine, cosine)
    return sine, cosine


def flat_row(tile, half):
    if tile < 2:
        return (2 * half + tile) * LANES
    return (4 + 3 * half + tile - 2) * LANES


def column_orders(wo_ref, z, mt_ref):
    lane = iota((8, LANES), 1)

    @pl.loop(0, COLS // LANES)
    def _(jb):
        half = jnp.where(jb < 4, jb // 2, (jb - 4) // 3)
        tile = jnp.where(jb < 4, jb % 2, 2 + (jb - 4) % 3)
        orders = jnp.zeros((8, LANES), jnp.int32)
        for n in range(8):
            plane = lax.rem(z + 4 + 8 * half + n, 16)
            base = plane * (4 * ROWS) + tile * TILE
            for k in range(16):
                value = wo_ref[base + (k // TILE) * ROWS + k % TILE]
                orders = jnp.where(lane == 16 * n + k, value, orders)
        mt_ref[pl.ds(jb, 1), :] = orders[0:1]


def longitude_tables(mt_ref, cos_xj, sin_xj, cos_jx, sin_jx, even_ref):
    @pl.loop(0, COLS // LANES)
    def _(jb):
        cols = pl.ds(pl.multiple_of(jb * LANES, LANES), LANES)
        mj = mt_ref[pl.ds(jb, 1), :]
        mf = mj.astype(F32)
        sb, cb = sin_cos(mf * iota((32, LANES), 0).astype(F32))
        sa, ca = sin_cos(mf * (32 * iota((24, LANES), 0)).astype(F32))
        for xa in range(XPAD // 32):
            rows = pl.ds(32 * xa, 32)
            if xa > 20:
                cos_xj[rows, cols] = jnp.zeros((32, LANES), BF16)
                sin_xj[rows, cols] = jnp.zeros((32, LANES), BF16)
                continue
            sa1, ca1 = sa[xa : xa + 1], ca[xa : xa + 1]
            c = ca1 * cb - sa1 * sb
            s = sa1 * cb + ca1 * sb
            if xa == 20:
                c = jnp.where(iota((32, LANES), 0) == 0, c, 0.0)
                s = jnp.where(iota((32, LANES), 0) == 0, s, 0.0)
            cos_xj[rows, cols] = c.astype(BF16)
            sin_xj[rows, cols] = s.astype(BF16)
        even = jnp.where(lax.rem(mj, 2) == 0, 1.0, 0.0)
        even_ref[cols, :] = jnp.broadcast_to(even, (LANES, LANES)).T
        for xb in range(XPAD // LANES):
            rows = pl.ds(xb * LANES, LANES)
            cos_jx[cols, rows] = cos_xj[rows, cols].T
            sin_jx[cols, rows] = sin_xj[rows, cols].T


def grid_lane(u):
    slot, v = u // 64, u % 64
    flux = jnp.where(slot == 0, v // 16, v // 8)
    s = jnp.where(slot == 0, v // 8 % 2, v // 4 % 2)
    level = jnp.where(slot == 0, v % 8, v % 4)
    return slot, flux, s, level, (slot == 0) | (v < 32)


def pick_fields():
    row, col = iota((256, 512), 0), iota((256, 512), 1)
    slot, level, s, part, field = row // 128, row // 16 % 8, row // 8 % 2, row // 4 % 2, row % 4
    c_part, side = col // 256, col // 128 % 2
    c_slot, flux, c_s, c_level, used = grid_lane(col % 128)
    wanted = jnp.where(side == 0, flux % 2, 2 + flux // 2)
    same = used & (slot == c_slot) & (s == c_s) & (level == c_level)
    same = same & (part == c_part) & (field == wanted)
    return jnp.where(same, 1.0, 0.0).astype(BF16)


def place_fluxes():
    row, col = iota((256, 256), 0), iota((256, 256), 1)
    part = row // 128
    slot, flux, s, level, used = grid_lane(row % 128)
    c_slot = col // 128
    c_level = jnp.where(c_slot == 0, col // 16 % 8, col // 16 % 4)
    same = used & (slot == c_slot) & (level == c_level) & (s == col // 8 % 2)
    same = same & (part == col // 4 % 2) & (flux == col % 4)
    return jnp.where(same, 1.0, 0.0).astype(BF16)


def kernel(
    wo_hbm, trunc_hbm, spec_ref, out_ref,
    wo_ref, trunc_ref, mt_ref,
    alpha_ref, both_ref, tab0, tab1, tab2,
    cos_xj, sin_xj, cos_jx, sin_jx, even_ref,
    gath, stage, send_fl, send_fh, recv_fl, recv_fh, send_bl, send_bh, recv_bl, recv_bh,
    flat0, flat1, x_re, x_im, acc_c, acc_s, h_c, h_s,
    partial, e1_recv, e2_send, e2_recv,
    in_sem, ready, own_sem, g_send, g_recv, c_send, c_recv,
    fl_ss, fl_rs, fh_ss, fh_rs, bl_ss, bl_rs, bh_ss, bh_rs,
    e1_ss, e1_rs, e2_ss, e2_rs,
):
    me = lax.axis_index("wave")
    lev = lax.axis_index("lev")
    y = lev // 2
    core = lev % 2
    partner = y * 2 + (1 - core)
    x = lax.rem(me, 4)
    z = me // 4
    tabs = (tab0, tab1, tab2)
    lane4 = iota((TILE, LANES), 1)

    inputs = (
        pltpu.make_async_copy(wo_hbm, wo_ref, in_sem.at[0]),
        pltpu.make_async_copy(trunc_hbm, trunc_ref, in_sem.at[1]),
    )
    for copy in inputs:
        copy.start()

    def z_peer(i):
        return lax.rem(me + 4 * i + WAVES, WAVES)

    def x_peer(i):
        return me - x + lax.rem(x + i, 4)

    barrier = pltpu.get_barrier_semaphore()
    for i in range(1, 4):
        pl.semaphore_signal(
            barrier, inc=1, device_id=(me, lax.rem(lev + 2 * i, LEVS)), device_id_type=MESH
        )
    pl.semaphore_signal(barrier, inc=1, device_id=(me, partner), device_id_type=MESH)
    for peer in (z_peer(1), z_peer(-1), x_peer(1), x_peer(2), x_peer(3)):
        pl.semaphore_signal(barrier, inc=1, device_id=(peer, lev), device_id_type=MESH)

    def say(step):
        reach = (1, 2, 4)
        if step < 3:
            peers = (z_peer(reach[step]), z_peer(-reach[step]))
        else:
            peers = (x_peer(1), x_peer(2), x_peer(3))
        for peer in peers:
            pl.semaphore_signal(ready.at[step], inc=1, device_id=(peer, lev), device_id_type=MESH)

    def hear(step):
        pl.semaphore_wait(ready.at[step], 2 if step < 3 else 3)

    for copy in inputs:
        copy.wait()
    lat0 = first_latitude(lev)
    orders = own_orders(wo_ref, me * ROWS)
    cosine, state = recurrence_start(wo_ref, me * ROWS, orders, lat0, alpha_ref, both_ref)
    flat1[...] = jnp.zeros_like(flat1)
    h_c[pl.ds(XROWS, XPAD - XROWS), :] = jnp.zeros((XPAD - XROWS, 256), BF16)
    h_s[pl.ds(XROWS, XPAD - XROWS), :] = jnp.zeros((XPAD - XROWS, 256), BF16)

    pl.semaphore_wait(barrier, 9)
    say(0)

    light_groups = tuple(range(HEAVY // 2, GROUPS))
    heavy_groups = tuple(range(HEAVY // 2))

    def piece(ref, level, g):
        return ref.at[level, pl.ds(2 * g, 2), :, pl.ds(0, WIDTHS[g])]

    def own_copy():
        return pltpu.make_async_copy(spec_ref.at[0], gath.at[lev], own_sem)

    def y_copy(i, g):
        return pltpu.make_async_remote_copy(
            piece(spec_ref, 0, g), piece(gath, lev, g), g_send.at[i, g], g_recv.at[i, g],
            device_id=(me, lax.rem(lev + 2 * i, LEVS)), device_id_type=MESH,
        )

    def core_copy(i, g):
        level = lax.rem(lev + LEVS - 2 * i, LEVS)
        src = piece(spec_ref, 0, g) if i == 0 else piece(gath, level, g)
        return pltpu.make_async_remote_copy(
            src, piece(gath, level, g), c_send.at[i, g], c_recv.at[i, g],
            device_id=(me, partner), device_id_type=MESH,
        )

    def pass_on(groups):
        for g in groups:
            for i in range(1, 4):
                y_copy(i, g).wait()
                core_copy(i, g).start()

    def gathered(groups):
        for g in groups:
            for i in range(4):
                core_copy(i, g).wait()

    for groups in (light_groups, heavy_groups):
        for g in groups:
            for i in range(1, 4):
                y_copy(i, g).start()
        for g in groups:
            core_copy(0, g).start()
    own_copy().start()

    angles = half_angles(lat0)[0:1]
    lane = iota((1, LANES), 1)
    cut = jnp.zeros((1, LANES), jnp.int32)
    for n in range(LANES):
        cut = jnp.where(lane == n, trunc_ref[lat0 + n], cut)
    area = (float(TOP) / LON) * (math.pi / TOP) * jnp.sin(angles)
    area = jnp.where(iota((1, LANES), 1) < 64 + 32 * core, area, 0.0)
    sign = jnp.where(iota((1, TOP), 1) % 2 == 0, 1.0, -1.0)

    def legendre_row(r):
        width = WIDTHS[r // 2]
        table = table_rows(tabs, r, width)
        coeff = gath[:, r, :, 0:width].astype(F32)
        both_signs = jnp.stack([coeff, coeff * sign[:, :width]], axis=1).reshape(LANES, width)
        fourier = jnp.dot(both_signs.astype(BF16), table, preferred_element_type=F32)
        order = wo_ref[me * ROWS + r]
        weight = jnp.where(order == 0, 1.0, 2.0)
        fourier = fourier * jnp.where(order < cut, weight, 0.0)
        stage[pl.ds(r // TILE * 512 + r % TILE, LANES, stride=TILE), :] = fourier.T

    def both_cores(main, extra, act):
        @pl.when(core == 0)
        def _():
            act(main)

        @pl.when(core == 1)
        def _():
            act(main + extra)

    def peer(half, t):
        return lax.rem(z + 4 + 8 * half + t // 4, 16) * 4 + lax.rem(t, 4)

    def send_half(bufs, half, main, extra):
        send, recv, ss, rs = bufs

        def start(count):
            @pl.loop(0, HALF, unroll=4)
            def _(t):
                to = peer(half, t)

                @pl.when(to != me)
                def _():
                    pltpu.make_async_remote_copy(
                        send.at[to, pl.ds(0, count)], recv.at[me, pl.ds(0, count)], ss, rs,
                        device_id=(to, lev), device_id_type=MESH,
                    ).start()

        both_cores(main, extra, start)
        if half == 1:
            recv[me] = send[me]

    def wait_all(bufs, main, extra):
        send, recv, ss, rs = bufs

        def wait(count):
            window = (pl.ds(0, WAVES - 1), pl.ds(0, count))
            pltpu.make_async_copy(send.at[window], send.at[window], ss).wait()
            pltpu.make_async_copy(recv.at[window], recv.at[window], rs).wait()

        both_cores(main, extra, wait)

    fl = (send_fl, recv_fl, fl_ss, fl_rs)
    fh = (send_fh, recv_fh, fh_ss, fh_rs)
    bl = (send_bl, recv_bl, bl_ss, bl_rs)
    bh = (send_bh, recv_bh, bh_ss, bh_rs)

    def pack(send, tiles, pairs):
        @pl.loop(0, WAVES, unroll=8)
        def _(w):
            for q, tile in enumerate(tiles):
                send[w, q] = stage[pl.ds(tile * 512 + TILE * w, TILE), :].astype(BF16)

        @pl.when(core == 1)
        def _():
            @pl.loop(0, HALF, unroll=8)
            def _(e):
                place = TILE * (WAVES + e)
                for q, (one, two) in enumerate(pairs):
                    first = stage[pl.ds(one * 512 + place, TILE), :]
                    second = pltpu.roll(stage[pl.ds(two * 512 + place, TILE), :], 64, 1)
                    q = len(tiles) + q
                    send[2 * e, q] = jnp.where(lane4 < 64, first, second).astype(BF16)
                    send[2 * e + 1, q] = jnp.where(lane4 < 64, second, first).astype(BF16)

    hear(0)
    say(1)
    state = recurrence_phase(0, cosine, state, alpha_ref, both_ref, tabs)
    hear(1)
    say(2)
    state = recurrence_phase(1, cosine, state, alpha_ref, both_ref, tabs)
    hear(2)
    say(3)
    pass_on(light_groups)
    recurrence_phase(2, cosine, state, alpha_ref, both_ref, tabs)
    own_copy().wait()
    gathered(light_groups)
    for r in range(HEAVY, ROWS):
        legendre_row(r)
    pack(send_fl, LIGHT_TILES, LIGHT_PAIRS)
    hear(3)
    send_half(fl, 0, 3, 2)
    send_half(fl, 1, 3, 2)

    pass_on(heavy_groups)
    gathered(heavy_groups)
    for r in range(HEAVY):
        legendre_row(r)
    pack(send_fh, HEAVY_TILES, HEAVY_PAIRS)
    send_half(fh, 0, 2, 1)
    send_half(fh, 1, 2, 1)

    column_orders(wo_ref, z, mt_ref)
    longitude_tables(mt_ref, cos_xj, sin_xj, cos_jx, sin_jx, even_ref)

    fields = pick_fields()

    def unpack(recv, tiles, pairs):
        odd = me % 2 == 1
        for half in range(2):

            @pl.loop(0, HALF, unroll=8)
            def _(t):
                for q, tile in enumerate(tiles):
                    place = pl.ds(flat_row(tile, half) + TILE * t, TILE)
                    flat0[place, :] = recv[peer(half, t), q].astype(F32)

            @pl.when(core == 1)
            def _():
                @pl.loop(0, HALF, unroll=8)
                def _(t):
                    for q, (one, two) in enumerate(pairs):
                        here = recv[peer(half, t), len(tiles) + q].astype(F32)
                        there = pltpu.roll(here, 64, 1)
                        place = pl.ds(flat_row(one, half) + TILE * t, TILE)
                        flat1[place, :] = jnp.where(odd, there, here)
                        if two != one:
                            place = pl.ds(flat_row(two, half) + TILE * t, TILE)
                            flat1[place, :] = jnp.where(odd, here, there)

    def build(first_row, count):
        @pl.loop(0, count // LANES)
        def _(b):
            rows = pl.ds(pl.multiple_of(first_row + b * LANES, LANES), LANES)
            raw = jnp.concatenate([flat0[rows, :], flat1[rows, :]], axis=1).astype(BF16)
            picked = jnp.dot(raw, fields, preferred_element_type=F32)
            even = even_ref[rows, :]
            even = jnp.concatenate([even, even], axis=1)
            for part, ref in ((0, x_re), (1, x_im)):
                both = picked[:, 256 * part : 256 * part + 256]
                evens = both * even
                ref[rows, :] = jnp.concatenate([evens, both - evens], axis=1).astype(BF16)

    heavy = pl.ds(0, HEAVY_COLS)
    light = pl.ds(HEAVY_COLS, COLS - HEAVY_COLS)

    wait_all(fl, 3, 2)
    unpack(recv_fl, LIGHT_TILES, LIGHT_PAIRS)
    build(HEAVY_COLS, COLS - HEAVY_COLS)

    @pl.loop(0, XROWS // XBLK)
    def _(b):
        rows = pl.ds(pl.multiple_of(b * XBLK, 16), XBLK)
        acc_c[rows, :] = jnp.dot(cos_xj[rows, light], x_re[light, :], preferred_element_type=F32)
        acc_s[rows, :] = jnp.dot(sin_xj[rows, light], x_im[light, :], preferred_element_type=F32)

    wait_all(fh, 2, 1)
    unpack(recv_fh, HEAVY_TILES, HEAVY_PAIRS)
    build(0, HEAVY_COLS)

    @pl.loop(0, XROWS // XBLK)
    def _(b):
        rows = pl.ds(pl.multiple_of(b * XBLK, 16), XBLK)
        c = acc_c[rows, :] + jnp.dot(
            cos_xj[rows, heavy], x_re[heavy, :], preferred_element_type=F32
        )
        s = acc_s[rows, :] + jnp.dot(
            sin_xj[rows, heavy], x_im[heavy, :], preferred_element_type=F32
        )
        c_sum, c_dif = c[:, :256] + c[:, 256:], c[:, :256] - c[:, 256:]
        s_sum, s_dif = s[:, :256] + s[:, 256:], s[:, :256] - s[:, 256:]

        def flux(g):
            return g[:, :128] * g[:, 128:]

        place = iota((XBLK, LANES), 0) + b * XBLK
        once = jnp.where((place == 0) | (place == LON // 4), 0.5, 1.0)
        f1 = flux(c_sum - s_sum) * once
        f2 = flux(c_sum + s_sum) * once
        f3 = flux(c_dif + s_dif) * once
        f4 = flux(c_dif - s_dif) * once
        near, far = f1 + f2, f3 + f4
        near_d, far_d = f2 - f1, f3 - f4
        h_c[rows, :] = jnp.concatenate([near + far, near - far], axis=1).astype(BF16)
        h_s[rows, :] = jnp.concatenate([near_d + far_d, near_d - far_d], axis=1).astype(BF16)

    places = place_fluxes()

    def direct(first_row, count):
        rows = pl.ds(first_row, count)
        c = jnp.dot(cos_jx[rows, :], h_c[...], preferred_element_type=F32)
        s = jnp.dot(sin_jx[rows, :], h_s[...], preferred_element_type=F32)
        even = even_ref[rows, :] > 0.5
        c = jnp.where(even, c[:, :128], c[:, 128:])
        s = jnp.where(even, s[:, :128], s[:, 128:])
        back = jnp.dot(
            jnp.concatenate([c, s], axis=1).astype(BF16), places, preferred_element_type=F32
        )
        flat0[rows, :] = back[:, :LANES]
        flat1[rows, :] = back[:, LANES:]

    def pack_back(send, half, tiles, pairs):
        @pl.loop(0, HALF, unroll=8)
        def _(t):
            for q, tile in enumerate(tiles):
                place = pl.ds(flat_row(tile, half) + TILE * t, TILE)
                send[peer(half, t), q] = flat0[place, :].astype(BF16)

        @pl.when(core == 1)
        def _():
            @pl.loop(0, HALF, unroll=8)
            def _(t):
                for q, (one, two) in enumerate(pairs):
                    first = flat1[pl.ds(flat_row(one, half) + TILE * t, TILE), :]
                    second = flat1[pl.ds(flat_row(two, half) + TILE * t, TILE), :]
                    both = jnp.where(lane4 < 64, first, second).astype(BF16)
                    send[peer(half, t), len(tiles) + q] = both

    for half in range(2):
        direct(half * 256, 256)
        pack_back(send_bh, half, HEAVY_TILES, HEAVY_PAIRS)
        send_half(bh, half, 2, 1)
    for half in range(2):
        direct(HEAVY_COLS + half * 384, 384)
        pack_back(send_bl, half, LIGHT_TILES, LIGHT_PAIRS)
        send_half(bl, half, 3, 2)

    def unpack_back(recv, tiles, pairs):
        @pl.loop(0, WAVES, unroll=8)
        def _(w):
            for q, tile in enumerate(tiles):
                stage[pl.ds(tile * 512 + TILE * w, TILE), :] = recv[w, q].astype(F32)

        @pl.when(core == 1)
        def _():
            @pl.loop(0, HALF, unroll=8)
            def _(e):
                place = TILE * (WAVES + e)
                for q, (one, two) in enumerate(pairs):
                    low = recv[2 * e, len(tiles) + q].astype(F32)
                    high = recv[2 * e + 1, len(tiles) + q].astype(F32)
                    first = jnp.where(lane4 < 64, low, pltpu.roll(high, 64, 1))
                    stage[pl.ds(one * 512 + place, TILE), :] = first
                    if two != one:
                        second = jnp.where(lane4 < 64, pltpu.roll(low, 64, 1), high)
                        stage[pl.ds(two * 512 + place, TILE), :] = second

    def e1_copy(g):
        window = (slice(None), pl.ds(2 * g, 2), slice(None), pl.ds(0, WIDTHS[g]))
        return pltpu.make_async_remote_copy(
            partial.at[(1 - core,) + window], e1_recv.at[window], e1_ss.at[g], e1_rs.at[g],
            device_id=(me, partner), device_id_type=MESH,
        )

    def e2_copy(i, g):
        to = lax.rem(y + i, 4)
        return pltpu.make_async_remote_copy(
            piece(e2_send, to, g), piece(e2_recv, i - 1, g), e2_ss.at[i, g], e2_rs.at[i, g],
            device_id=(me, to * 2 + core), device_id_type=MESH,
        )

    def add_cores(g):
        e1_copy(g).wait()
        for r in (2 * g, 2 * g + 1):
            for q in range(4):
                mine = partial[core, q, r, :, 0 : WIDTHS[g]].astype(F32)
                other = e1_recv[q, r, :, 0 : WIDTHS[g]].astype(F32)
                e2_send[q, r, :, 0 : WIDTHS[g]] = (mine + other).astype(BF16)
        for i in (2, 1, 3):
            e2_copy(i, g).start()

    def flux_rows(g):
        width = WIDTHS[g]
        for r in (2 * g, 2 * g + 1):
            table = table_rows(tabs, r, width)
            order = wo_ref[me * ROWS + r]
            weight = jnp.where(order == 0, 1.0, 0.5)
            factor = jnp.where(order < cut, area * weight, 0.0)
            back = stage[pl.ds(r // TILE * 512 + r % TILE, LANES, stride=TILE), :]
            sums = lax.dot_general(
                (back.T * factor).astype(BF16), table, (((1,), (1,)), ((), ())),
                preferred_element_type=F32,
            )
            sums = sums.reshape(LEVS, 2, 8, width)
            sums = (sums[:, 0] + sums[:, 1] * sign[:, :width]).astype(BF16)
            for l in range(LEVS):
                partial[l % 2, l // 2, r, :, 0:width] = sums[l]
        e1_copy(g).start()

    wait_all(bh, 2, 1)
    unpack_back(recv_bh, HEAVY_TILES, HEAVY_PAIRS)
    for g in heavy_groups:
        flux_rows(g)
    for g in heavy_groups:
        add_cores(g)
    wait_all(bl, 3, 2)
    unpack_back(recv_bl, LIGHT_TILES, LIGHT_PAIRS)
    for g in light_groups:
        flux_rows(g)
    for g in light_groups:
        add_cores(g)
    for g in range(GROUPS):
        width = WIDTHS[g]
        for i in range(1, 4):
            e2_copy(i, g).wait()
        for r in (2 * g, 2 * g + 1):
            total = e2_send[y, r, :, 0:width].astype(F32)
            for i in range(3):
                total = total + e2_recv[i, r, :, 0:width].astype(F32)
            out_ref[0, r, :, 0:width] = total.astype(BF16)
            if width < TOP:
                out_ref[0, r, :, width:TOP] = jnp.zeros((8, TOP - width), BF16)


def on_device(spectra, wave_order, truncation):
    anywhere = pl.BlockSpec(memory_space=pl.ANY)
    vmem = pl.BlockSpec(memory_space=pltpu.VMEM)
    dma = pltpu.SemaphoreType.DMA
    message = lambda tiles: pltpu.VMEM((WAVES, tiles, TILE, LANES), BF16)
    flux = pl.pallas_call(
        kernel,
        out_shape=jax.ShapeDtypeStruct((1, ROWS, 8, TOP), BF16),
        in_specs=[anywhere] * 3,
        out_specs=vmem,
        scratch_shapes=[
            pltpu.SMEM((TOP,), jnp.int32),
            pltpu.SMEM((TOP,), jnp.int32),
            pltpu.VMEM((16, LANES), jnp.int32),
            pltpu.VMEM((10, ROWS_PAD, LANES), F32),
            pltpu.VMEM((10, ROWS_PAD, LANES), F32),
            pltpu.VMEM((8 * TAB_STRIDE[0], LANES), F32),
            pltpu.VMEM((8 * TAB_STRIDE[1], LANES), F32),
            pltpu.VMEM((8 * TAB_STRIDE[2], LANES), F32),
            pltpu.VMEM((XPAD, COLS), BF16),
            pltpu.VMEM((XPAD, COLS), BF16),
            pltpu.VMEM((COLS, XPAD), BF16),
            pltpu.VMEM((COLS, XPAD), BF16),
            pltpu.VMEM((COLS, LANES), F32),
            pltpu.VMEM((LEVS, ROWS, 8, TOP), BF16),
            pltpu.VMEM((LANES * ROWS, LANES), F32),
            message(5), message(3), message(5), message(3),
            message(5), message(3), message(5), message(3),
            pltpu.VMEM((COLS, LANES), F32),
            pltpu.VMEM((COLS, LANES), F32),
            pltpu.VMEM((COLS, 512), BF16),
            pltpu.VMEM((COLS, 512), BF16),
            pltpu.VMEM((XROWS, 512), F32),
            pltpu.VMEM((XROWS, 512), F32),
            pltpu.VMEM((XPAD, 256), BF16),
            pltpu.VMEM((XPAD, 256), BF16),
            pltpu.VMEM((2, 4, ROWS, 8, TOP), BF16),
            pltpu.VMEM((4, ROWS, 8, TOP), BF16),
            pltpu.VMEM((4, ROWS, 8, TOP), BF16),
            pltpu.VMEM((3, ROWS, 8, TOP), BF16),
            dma((2,)),
            pltpu.SemaphoreType.REGULAR((4,)),
            dma,
            dma((4, GROUPS)), dma((4, GROUPS)), dma((4, GROUPS)), dma((4, GROUPS)),
            dma, dma, dma, dma, dma, dma, dma, dma,
            dma((GROUPS,)), dma((GROUPS,)), dma((4, GROUPS)), dma((4, GROUPS)),
        ],
        compiler_params=pltpu.CompilerParams(
            collective_id=0, has_side_effects=True, vmem_limit_bytes=60 * 2**20
        ),
        name="flux_transform",
    )(wave_order, truncation, spectra)
    return flux.astype(F32)


def solution(mesh):
    return jax.shard_map(
        on_device,
        mesh=mesh,
        in_specs=(P("lev", "wave", None, None), P(), P()),
        out_specs=P("lev", "wave", None, None),
        check_vma=False,
    )
```

```python
import functools
import math

import jax
import jax.numpy as jnp
from jax import lax
from jax.experimental import pallas as pl
from jax.experimental.pallas import tpu as pltpu
from jax.sharding import PartitionSpec as P

MESH = pl.DeviceIdType.MESH
F32 = jnp.float32
BF16 = jnp.bfloat16

TOP = 1280
LON = 2560
ROWS = 20
ROWS_PAD = 24
WAVES = 64
LEVS = 8
LANES = 128
RESCALE = 16
GROUPS = ROWS // 4
WIDTHS = tuple(TOP - 2 * LANES * g for g in range(GROUPS))
TAB_LEN = (1280, 768, 256)
TAB_STRIDE = (1288, 776, 264)
COLS = WAVES * ROWS
HEAVY_COLS = WAVES * 8
XROWS = 672
XPAD = 768
XBLK = 224
TILE = 4
HEAVY = (0, 1)
MID = (2, 3)
LIGHT = (4,)
HALF = WAVES // 2


def iota(shape, dim):
    return lax.broadcasted_iota(jnp.int32, shape, dim)


def first_latitude(lev):
    return 160 * (lev // 2) + 64 * (lev % 2)


def half_angles(lat0):
    lat = iota((8, LANES), 1) + lat0
    return math.pi / TOP * (lat.astype(F32) + 0.5)


def own_orders(wo_ref, base):
    rows = iota((ROWS_PAD, LANES), 0)
    orders = jnp.full((ROWS_PAD, LANES), TOP, jnp.int32)
    for r in range(ROWS):
        orders = jnp.where(rows == r, wo_ref[base + r], orders)
    return orders


def recurrence_start(wo_ref, base, orders, lat0, alpha_ref, both_ref):
    place = iota((16, LANES), 0) * LANES + iota((16, LANES), 1)
    j = jnp.maximum(place, 1).astype(F32)
    terms = jnp.where((place >= 1) & (place < TOP), jnp.log((2.0 * j + 1.0) / (2.0 * j)), 0.0)
    rows = iota((ROWS_PAD, LANES), 0)
    logs = jnp.zeros((ROWS_PAD, LANES), F32)
    for r in range(ROWS):
        part = jnp.where(place <= wo_ref[base + r], terms, 0.0)
        total = jnp.sum(jnp.sum(part, axis=0, keepdims=True), axis=1, keepdims=True)
        logs = jnp.where(rows == r, total, logs)
    order = orders.astype(F32)
    angles = half_angles(lat0)
    cosine = jnp.cos(angles)
    log_sine = jnp.log(jnp.sin(angles))
    for kb in range(TOP // LANES):
        k = iota((ROWS_PAD, LANES), 1) + (kb * LANES + 1)
        kf = k.astype(F32)
        n = order + kf
        alpha = jnp.sqrt((4.0 * n * n - 1.0) / (kf * (n + order)))
        low = n - 1.0
        beta = jnp.sqrt(
            (kf - 1.0) * (kf - 1.0 + 2.0 * order) / jnp.maximum(4.0 * low * low - 1.0, 1.0)
        )
        kept = orders + k < TOP
        alpha_ref[kb] = jnp.where(kept, alpha, 0.0)
        both_ref[kb] = jnp.where(kept, alpha * beta, 0.0)
    state = []
    for g in range(3):
        part = slice(8 * g, 8 * g + 8)
        scale = 0.5 * math.log(0.5) + 0.5 * logs[part] + order[part] * log_sine
        state += [jnp.zeros((8, LANES), F32), jnp.ones((8, LANES), F32), scale]
    return cosine, state


def recurrence_phase(phase, cosine, state, alpha_ref, both_ref, tabs):
    live, start, stop = ((3, 0, 2), (2, 2, 6), (1, 6, 10))[phase]

    def block(kb, flat):
        st = [tuple(flat[3 * g : 3 * g + 3]) for g in range(live)]
        alpha = alpha_ref[kb]
        both = both_ref[kb]
        for i in range(LANES):
            if i % RESCALE == 0:
                factor = [jnp.exp(s[2]) for s in st]
            for g in range(live):
                prev, cur, scale = st[g]
                rows = pl.ds(kb * LANES + i, 8, stride=TAB_STRIDE[g])
                tabs[g][rows, :] = cur * factor[g]
                part = slice(8 * g, 8 * g + 8)
                fresh = (alpha[part, i : i + 1] * cosine) * cur - both[part, i : i + 1] * prev
                st[g] = (cur, fresh, scale)
            if i % RESCALE == RESCALE - 1:
                for g in range(live):
                    prev, cur, scale = st[g]
                    big = jnp.maximum(jnp.maximum(jnp.abs(prev), jnp.abs(cur)), 1e-30)
                    inv = 1.0 / big
                    st[g] = (prev * inv, cur * inv, scale + jnp.log(big))
        return tuple(v for s in st for v in s)

    return list(lax.fori_loop(start, stop, block, tuple(state[: 3 * live])))


def table_rows(tabs, r, width):
    g = r // 8
    return tabs[g][pl.ds((r % 8) * TAB_STRIDE[g], width), :].astype(BF16)


def sin_cos(phase):
    turns = jnp.floor(phase * (1.0 / LON))
    phase = phase - turns * LON
    quarter = jnp.floor(phase * (4.0 / LON) + 0.5)
    t = (phase - quarter * (LON // 4)) * (2.0 * math.pi / LON)
    t2 = t * t
    s = t * (1.0 + t2 * (-1.0 / 6 + t2 * (1.0 / 120 + t2 * (-1.0 / 5040 + t2 * (1.0 / 362880)))))
    c = 1.0 + t2 * (-0.5 + t2 * (1.0 / 24 + t2 * (-1.0 / 720 + t2 * (1.0 / 40320))))
    odd = (quarter == 1.0) | (quarter == 3.0)
    sine = jnp.where(odd, c, s)
    cosine = jnp.where(odd, s, c)
    sine = jnp.where((quarter == 2.0) | (quarter == 3.0), -sine, sine)
    cosine = jnp.where((quarter == 1.0) | (quarter == 2.0), -cosine, cosine)
    return sine, cosine


def flat_row(tile, half):
    if tile < 2:
        return (2 * half + tile) * LANES
    return (4 + 3 * half + tile - 2) * LANES


def column_orders(wo_ref, z, mt_ref):
    lane = iota((8, LANES), 1)

    @pl.loop(0, COLS // LANES)
    def _(jb):
        half = jnp.where(jb < 4, jb // 2, (jb - 4) // 3)
        tile = jnp.where(jb < 4, jb % 2, 2 + (jb - 4) % 3)
        orders = jnp.zeros((8, LANES), jnp.int32)
        for n in range(8):
            plane = lax.rem(z + 4 + 8 * half + n, 16)
            base = plane * (4 * ROWS) + tile * TILE
            for k in range(16):
                value = wo_ref[base + (k // TILE) * ROWS + k % TILE]
                orders = jnp.where(lane == 16 * n + k, value, orders)
        mt_ref[pl.ds(jb, 1), :] = orders[0:1]


def longitude_tables(mt_ref, cos_xj, sin_xj, cos_jx, sin_jx, even_ref):
    @pl.loop(0, COLS // LANES)
    def _(jb):
        cols = pl.ds(pl.multiple_of(jb * LANES, LANES), LANES)
        mj = mt_ref[pl.ds(jb, 1), :]
        mf = mj.astype(F32)
        sb, cb = sin_cos(mf * iota((32, LANES), 0).astype(F32))
        sa, ca = sin_cos(mf * (32 * iota((24, LANES), 0)).astype(F32))
        for xa in range(XPAD // 32):
            rows = pl.ds(32 * xa, 32)
            if xa > 20:
                cos_xj[rows, cols] = jnp.zeros((32, LANES), BF16)
                sin_xj[rows, cols] = jnp.zeros((32, LANES), BF16)
                continue
            sa1, ca1 = sa[xa : xa + 1], ca[xa : xa + 1]
            c = ca1 * cb - sa1 * sb
            s = sa1 * cb + ca1 * sb
            if xa == 20:
                c = jnp.where(iota((32, LANES), 0) == 0, c, 0.0)
                s = jnp.where(iota((32, LANES), 0) == 0, s, 0.0)
            cos_xj[rows, cols] = c.astype(BF16)
            sin_xj[rows, cols] = s.astype(BF16)
        even = jnp.where(lax.rem(mj, 2) == 0, 1.0, 0.0)
        even_ref[cols, :] = jnp.broadcast_to(even, (LANES, LANES)).T
        for xb in range(XPAD // LANES):
            rows = pl.ds(xb * LANES, LANES)
            cos_jx[cols, rows] = cos_xj[rows, cols].T
            sin_jx[cols, rows] = sin_xj[rows, cols].T


def grid_lane(u):
    slot, v = u // 64, u % 64
    flux = jnp.where(slot == 0, v // 16, v // 8)
    s = jnp.where(slot == 0, v // 8 % 2, v // 4 % 2)
    level = jnp.where(slot == 0, v % 8, v % 4)
    return slot, flux, s, level, (slot == 0) | (v < 32)


def pick_fields():
    row, col = iota((256, 512), 0), iota((256, 512), 1)
    slot, level, s, part, field = row // 128, row // 16 % 8, row // 8 % 2, row // 4 % 2, row % 4
    c_part, side = col // 256, col // 128 % 2
    c_slot, flux, c_s, c_level, used = grid_lane(col % 128)
    wanted = jnp.where(side == 0, flux % 2, 2 + flux // 2)
    same = used & (slot == c_slot) & (s == c_s) & (level == c_level)
    same = same & (part == c_part) & (field == wanted)
    return jnp.where(same, 1.0, 0.0).astype(BF16)


def place_fluxes():
    row, col = iota((256, 256), 0), iota((256, 256), 1)
    part = row // 128
    slot, flux, s, level, used = grid_lane(row % 128)
    c_slot = col // 128
    c_level = jnp.where(c_slot == 0, col // 16 % 8, col // 16 % 4)
    same = used & (slot == c_slot) & (level == c_level) & (s == col // 8 % 2)
    same = same & (part == col // 4 % 2) & (flux == col % 4)
    return jnp.where(same, 1.0, 0.0).astype(BF16)


def kernel(
    wo_hbm, trunc_hbm, spec_ref, out_ref,
    wo_ref, trunc_ref, mt_ref,
    alpha_ref, both_ref, tab0, tab1, tab2,
    cos_xj, sin_xj, cos_jx, sin_jx, even_ref,
    gath, stage,
    send_fl, send_fm, send_fh, recv_fl, recv_fm, recv_fh,
    send_bl, send_bm, send_bh, recv_bl, recv_bm, recv_bh,
    flat0, flat1, x_re, x_im, acc_c, acc_s, h_c, h_s,
    partial, e1_recv, e2_send, e2_recv,
    in_sem, ready, own_sem, g_send, g_recv, c_send, c_recv,
    f_ss, f_rs, b_ss, b_rs,
    e1_ss, e1_rs, e2_ss, e2_rs,
):
    me = lax.axis_index("wave")
    lev = lax.axis_index("lev")
    y = lev // 2
    core = lev % 2
    partner = y * 2 + (1 - core)
    x = lax.rem(me, 4)
    z = me // 4
    tabs = (tab0, tab1, tab2)
    lane4 = iota((TILE, LANES), 1)

    inputs = (
        pltpu.make_async_copy(wo_hbm, wo_ref, in_sem.at[0]),
        pltpu.make_async_copy(trunc_hbm, trunc_ref, in_sem.at[1]),
    )
    for copy in inputs:
        copy.start()

    def z_peer(i):
        return lax.rem(me + 4 * i + WAVES, WAVES)

    def x_peer(i):
        return me - x + lax.rem(x + i, 4)

    barrier = pltpu.get_barrier_semaphore()
    for i in range(1, 4):
        pl.semaphore_signal(
            barrier, inc=1, device_id=(me, lax.rem(lev + 2 * i, LEVS)), device_id_type=MESH
        )
    pl.semaphore_signal(barrier, inc=1, device_id=(me, partner), device_id_type=MESH)
    for peer in (z_peer(1), z_peer(-1), x_peer(1), x_peer(2), x_peer(3)):
        pl.semaphore_signal(barrier, inc=1, device_id=(peer, lev), device_id_type=MESH)

    def say(step):
        reach = (1, 2, 4)
        if step < 3:
            peers = (z_peer(reach[step]), z_peer(-reach[step]))
        else:
            peers = (x_peer(1), x_peer(2), x_peer(3))
        for peer in peers:
            pl.semaphore_signal(ready.at[step], inc=1, device_id=(peer, lev), device_id_type=MESH)

    def hear(step):
        pl.semaphore_wait(ready.at[step], 2 if step < 3 else 3)

    for copy in inputs:
        copy.wait()
    lat0 = first_latitude(lev)
    orders = own_orders(wo_ref, me * ROWS)
    cosine, state = recurrence_start(wo_ref, me * ROWS, orders, lat0, alpha_ref, both_ref)
    flat1[...] = jnp.zeros_like(flat1)
    h_c[pl.ds(XROWS, XPAD - XROWS), :] = jnp.zeros((XPAD - XROWS, 256), BF16)
    h_s[pl.ds(XROWS, XPAD - XROWS), :] = jnp.zeros((XPAD - XROWS, 256), BF16)

    state = recurrence_phase(0, cosine, state, alpha_ref, both_ref, tabs)
    pl.semaphore_wait(barrier, 9)
    say(0)

    def piece(ref, level, g):
        return ref.at[level, pl.ds(4 * g, 4), :, pl.ds(0, WIDTHS[g])]

    def own_copy():
        return pltpu.make_async_copy(spec_ref.at[0], gath.at[lev], own_sem)

    def y_copy(i, g):
        return pltpu.make_async_remote_copy(
            piece(spec_ref, 0, g), piece(gath, lev, g), g_send.at[i, g], g_recv.at[i, g],
            device_id=(me, lax.rem(lev + 2 * i, LEVS)), device_id_type=MESH,
        )

    def core_copy(i, g):
        level = lax.rem(lev + LEVS - 2 * i, LEVS)
        src = piece(spec_ref, 0, g) if i == 0 else piece(gath, level, g)
        return pltpu.make_async_remote_copy(
            src, piece(gath, level, g), c_send.at[i, g], c_recv.at[i, g],
            device_id=(me, partner), device_id_type=MESH,
        )

    def pass_on(groups):
        for g in groups:
            for i in range(1, 4):
                y_copy(i, g).wait()
                core_copy(i, g).start()

    def gathered(groups):
        for g in groups:
            for i in range(4):
                core_copy(i, g).wait()

    for groups in (LIGHT, MID, HEAVY):
        for g in groups:
            for i in (2, 1, 3):
                y_copy(i, g).start()
        for g in groups:
            core_copy(0, g).start()
        if groups == LIGHT:
            own_copy().start()
            hear(0)
            say(1)

    angles = half_angles(lat0)[0:1]
    lane = iota((1, LANES), 1)
    cut = jnp.zeros((1, LANES), jnp.int32)
    for n in range(LANES):
        cut = jnp.where(lane == n, trunc_ref[lat0 + n], cut)
    area = (float(TOP) / LON) * (math.pi / TOP) * jnp.sin(angles)
    area = jnp.where(iota((1, LANES), 1) < 64 + 32 * core, area, 0.0)
    sign = jnp.where(iota((1, TOP), 1) % 2 == 0, 1.0, -1.0)

    def legendre_row(r):
        width = WIDTHS[r // 4]
        table = table_rows(tabs, r, width)
        coeff = gath[:, r, :, 0:width].astype(F32)
        both_signs = jnp.stack([coeff, coeff * sign[:, :width]], axis=1).reshape(LANES, width)
        fourier = jnp.dot(both_signs.astype(BF16), table, preferred_element_type=F32)
        order = wo_ref[me * ROWS + r]
        weight = jnp.where(order == 0, 1.0, 2.0)
        fourier = fourier * jnp.where(order < cut, weight, 0.0)
        stage[pl.ds(r // TILE * 512 + r % TILE, LANES, stride=TILE), :] = fourier.T

    def both_cores(tiles, act):
        @pl.when(core == 0)
        def _():
            act(len(tiles))

        @pl.when(core == 1)
        def _():
            act(len(tiles) + 1)

    def peer(half, t):
        return lax.rem(z + 4 + 8 * half + t // 4, 16) * 4 + lax.rem(t, 4)

    def send_half(bufs, half):
        send, recv, ss, rs, tiles = bufs

        def start(count):
            @pl.loop(0, HALF, unroll=4)
            def _(t):
                to = peer(half, t)

                @pl.when(to != me)
                def _():
                    pltpu.make_async_remote_copy(
                        send.at[to, pl.ds(0, count)], recv.at[me, pl.ds(0, count)], ss, rs,
                        device_id=(to, lev), device_id_type=MESH,
                    ).start()

        both_cores(tiles, start)
        if half == 1:
            recv[me] = send[me]

    def wait_all(bufs):
        send, recv, ss, rs, tiles = bufs

        def wait(count):
            window = (pl.ds(0, WAVES - 1), pl.ds(0, count))
            pltpu.make_async_copy(send.at[window], send.at[window], ss).wait()
            pltpu.make_async_copy(recv.at[window], recv.at[window], rs).wait()

        both_cores(tiles, wait)

    fl = (send_fl, recv_fl, f_ss.at[0], f_rs.at[0], LIGHT)
    fm = (send_fm, recv_fm, f_ss.at[1], f_rs.at[1], MID)
    fh = (send_fh, recv_fh, f_ss.at[2], f_rs.at[2], HEAVY)
    bl = (send_bl, recv_bl, b_ss.at[0], b_rs.at[0], LIGHT)
    bm = (send_bm, recv_bm, b_ss.at[1], b_rs.at[1], MID)
    bh = (send_bh, recv_bh, b_ss.at[2], b_rs.at[2], HEAVY)

    def pack(bufs):
        send, tiles = bufs[0], bufs[4]
        one, two = tiles[0], tiles[-1]

        @pl.loop(0, WAVES, unroll=8)
        def _(w):
            for q, tile in enumerate(tiles):
                send[w, q] = stage[pl.ds(tile * 512 + TILE * w, TILE), :].astype(BF16)

        @pl.when(core == 1)
        def _():
            @pl.loop(0, HALF, unroll=8)
            def _(e):
                place = TILE * (WAVES + e)
                q = len(tiles)
                first = stage[pl.ds(one * 512 + place, TILE), :]
                second = pltpu.roll(stage[pl.ds(two * 512 + place, TILE), :], 64, 1)
                send[2 * e, q] = jnp.where(lane4 < 64, first, second).astype(BF16)
                send[2 * e + 1, q] = jnp.where(lane4 < 64, second, first).astype(BF16)

    hear(1)
    say(2)
    state = recurrence_phase(1, cosine, state, alpha_ref, both_ref, tabs)
    hear(2)
    say(3)
    pass_on(LIGHT)
    recurrence_phase(2, cosine, state, alpha_ref, both_ref, tabs)
    own_copy().wait()
    for bufs in (fl, fm, fh):
        groups = bufs[4]
        if groups != LIGHT:
            pass_on(groups)
        gathered(groups)
        for g in groups:
            for r in range(4 * g, 4 * g + 4):
                legendre_row(r)
        pack(bufs)
        if groups == LIGHT:
            hear(3)
        send_half(bufs, 0)
        send_half(bufs, 1)

    column_orders(wo_ref, z, mt_ref)
    longitude_tables(mt_ref, cos_xj, sin_xj, cos_jx, sin_jx, even_ref)

    fields = pick_fields()

    def unpack(bufs):
        recv, tiles = bufs[1], bufs[4]
        one, two = tiles[0], tiles[-1]
        odd = me % 2 == 1
        for half in range(2):

            @pl.loop(0, HALF, unroll=8)
            def _(t):
                for q, tile in enumerate(tiles):
                    place = pl.ds(flat_row(tile, half) + TILE * t, TILE)
                    flat0[place, :] = recv[peer(half, t), q].astype(F32)

            @pl.when(core == 1)
            def _():
                @pl.loop(0, HALF, unroll=8)
                def _(t):
                    here = recv[peer(half, t), len(tiles)].astype(F32)
                    there = pltpu.roll(here, 64, 1)
                    place = pl.ds(flat_row(one, half) + TILE * t, TILE)
                    flat1[place, :] = jnp.where(odd, there, here)
                    if two != one:
                        place = pl.ds(flat_row(two, half) + TILE * t, TILE)
                        flat1[place, :] = jnp.where(odd, here, there)

    def build(first_row, count):
        @pl.loop(0, count // LANES)
        def _(b):
            rows = pl.ds(pl.multiple_of(first_row + b * LANES, LANES), LANES)
            raw = jnp.concatenate([flat0[rows, :], flat1[rows, :]], axis=1).astype(BF16)
            picked = jnp.dot(raw, fields, preferred_element_type=F32)
            even = even_ref[rows, :]
            even = jnp.concatenate([even, even], axis=1)
            for part, ref in ((0, x_re), (1, x_im)):
                both = picked[:, 256 * part : 256 * part + 256]
                evens = both * even
                ref[rows, :] = jnp.concatenate([evens, both - evens], axis=1).astype(BF16)

    heavy = pl.ds(0, HEAVY_COLS)
    light = pl.ds(HEAVY_COLS, COLS - HEAVY_COLS)

    wait_all(fl)
    unpack(fl)
    wait_all(fm)
    unpack(fm)
    build(HEAVY_COLS, COLS - HEAVY_COLS)

    @pl.loop(0, XROWS // XBLK)
    def _(b):
        rows = pl.ds(pl.multiple_of(b * XBLK, 16), XBLK)
        acc_c[rows, :] = jnp.dot(cos_xj[rows, light], x_re[light, :], preferred_element_type=F32)
        acc_s[rows, :] = jnp.dot(sin_xj[rows, light], x_im[light, :], preferred_element_type=F32)

    wait_all(fh)
    unpack(fh)
    build(0, HEAVY_COLS)

    @pl.loop(0, XROWS // XBLK)
    def _(b):
        rows = pl.ds(pl.multiple_of(b * XBLK, 16), XBLK)
        c = acc_c[rows, :] + jnp.dot(
            cos_xj[rows, heavy], x_re[heavy, :], preferred_element_type=F32
        )
        s = acc_s[rows, :] + jnp.dot(
            sin_xj[rows, heavy], x_im[heavy, :], preferred_element_type=F32
        )
        c_sum, c_dif = c[:, :256] + c[:, 256:], c[:, :256] - c[:, 256:]
        s_sum, s_dif = s[:, :256] + s[:, 256:], s[:, :256] - s[:, 256:]

        def flux(g):
            return g[:, :128] * g[:, 128:]

        place = iota((XBLK, LANES), 0) + b * XBLK
        once = jnp.where((place == 0) | (place == LON // 4), 0.5, 1.0)
        f1 = flux(c_sum - s_sum) * once
        f2 = flux(c_sum + s_sum) * once
        f3 = flux(c_dif + s_dif) * once
        f4 = flux(c_dif - s_dif) * once
        near, far = f1 + f2, f3 + f4
        near_d, far_d = f2 - f1, f3 - f4
        h_c[rows, :] = jnp.concatenate([near + far, near - far], axis=1).astype(BF16)
        h_s[rows, :] = jnp.concatenate([near_d + far_d, near_d - far_d], axis=1).astype(BF16)

    places = place_fluxes()

    def direct(first_row, count):
        rows = pl.ds(first_row, count)
        c = jnp.dot(cos_jx[rows, :], h_c[...], preferred_element_type=F32)
        s = jnp.dot(sin_jx[rows, :], h_s[...], preferred_element_type=F32)
        even = even_ref[rows, :] > 0.5
        c = jnp.where(even, c[:, :128], c[:, 128:])
        s = jnp.where(even, s[:, :128], s[:, 128:])
        back = jnp.dot(
            jnp.concatenate([c, s], axis=1).astype(BF16), places, preferred_element_type=F32
        )
        flat0[rows, :] = back[:, :LANES]
        flat1[rows, :] = back[:, LANES:]

    def pack_back(bufs, half):
        send, tiles = bufs[0], bufs[4]
        one, two = tiles[0], tiles[-1]

        @pl.loop(0, HALF, unroll=8)
        def _(t):
            for q, tile in enumerate(tiles):
                place = pl.ds(flat_row(tile, half) + TILE * t, TILE)
                send[peer(half, t), q] = flat0[place, :].astype(BF16)

        @pl.when(core == 1)
        def _():
            @pl.loop(0, HALF, unroll=8)
            def _(t):
                first = flat1[pl.ds(flat_row(one, half) + TILE * t, TILE), :]
                second = flat1[pl.ds(flat_row(two, half) + TILE * t, TILE), :]
                both = jnp.where(lane4 < 64, first, second).astype(BF16)
                send[peer(half, t), len(tiles)] = both

    for half in range(2):
        direct(half * 256, 256)
        pack_back(bh, half)
        send_half(bh, half)
    for half in range(2):
        direct(HEAVY_COLS + half * 384, 384)
        pack_back(bm, half)
        send_half(bm, half)
    for half in range(2):
        pack_back(bl, half)
        send_half(bl, half)

    def unpack_back(bufs):
        recv, tiles = bufs[1], bufs[4]
        one, two = tiles[0], tiles[-1]

        @pl.loop(0, WAVES, unroll=8)
        def _(w):
            for q, tile in enumerate(tiles):
                stage[pl.ds(tile * 512 + TILE * w, TILE), :] = recv[w, q].astype(F32)

        @pl.when(core == 1)
        def _():
            @pl.loop(0, HALF, unroll=8)
            def _(e):
                place = TILE * (WAVES + e)
                low = recv[2 * e, len(tiles)].astype(F32)
                high = recv[2 * e + 1, len(tiles)].astype(F32)
                first = jnp.where(lane4 < 64, low, pltpu.roll(high, 64, 1))
                stage[pl.ds(one * 512 + place, TILE), :] = first
                if two != one:
                    second = jnp.where(lane4 < 64, pltpu.roll(low, 64, 1), high)
                    stage[pl.ds(two * 512 + place, TILE), :] = second

    def e1_copy(g):
        window = (slice(None), pl.ds(4 * g, 4), slice(None), pl.ds(0, WIDTHS[g]))
        return pltpu.make_async_remote_copy(
            partial.at[(1 - core,) + window], e1_recv.at[window], e1_ss.at[g], e1_rs.at[g],
            device_id=(me, partner), device_id_type=MESH,
        )

    def e2_copy(i, g):
        to = lax.rem(y + i, 4)
        return pltpu.make_async_remote_copy(
            piece(e2_send, to, g), piece(e2_recv, i - 1, g), e2_ss.at[i, g], e2_rs.at[i, g],
            device_id=(me, to * 2 + core), device_id_type=MESH,
        )

    def add_cores(g):
        e1_copy(g).wait()
        for r in range(4 * g, 4 * g + 4):
            for q in range(4):
                mine = partial[core, q, r, :, 0 : WIDTHS[g]].astype(F32)
                other = e1_recv[q, r, :, 0 : WIDTHS[g]].astype(F32)
                e2_send[q, r, :, 0 : WIDTHS[g]] = (mine + other).astype(BF16)
        for i in (2, 1, 3):
            e2_copy(i, g).start()

    def flux_rows(g):
        width = WIDTHS[g]
        for r in range(4 * g, 4 * g + 4):
            table = table_rows(tabs, r, width)
            order = wo_ref[me * ROWS + r]
            weight = jnp.where(order == 0, 1.0, 0.5)
            factor = jnp.where(order < cut, area * weight, 0.0)
            back = stage[pl.ds(r // TILE * 512 + r % TILE, LANES, stride=TILE), :]
            sums = lax.dot_general(
                (back.T * factor).astype(BF16), table, (((1,), (1,)), ((), ())),
                preferred_element_type=F32,
            )
            sums = sums.reshape(LEVS, 2, 8, width)
            sums = (sums[:, 0] + sums[:, 1] * sign[:, :width]).astype(BF16)
            for l in range(LEVS):
                partial[l % 2, l // 2, r, :, 0:width] = sums[l]
        e1_copy(g).start()

    def finish(g):
        width = WIDTHS[g]
        for i in range(1, 4):
            e2_copy(i, g).wait()
        for r in range(4 * g, 4 * g + 4):
            total = e2_send[y, r, :, 0:width].astype(F32)
            for i in range(3):
                total = total + e2_recv[i, r, :, 0:width].astype(F32)
            out_ref[0, r, :, 0:width] = total.astype(BF16)
            if width < TOP:
                out_ref[0, r, :, width:TOP] = jnp.zeros((8, TOP - width), BF16)

    for bufs in (bh, bm, bl):
        groups = bufs[4]
        wait_all(bufs)
        unpack_back(bufs)
        for g in groups:
            flux_rows(g)
        for g in groups:
            add_cores(g)
    for g in range(GROUPS):
        finish(g)


def on_device(spectra, wave_order, truncation):
    anywhere = pl.BlockSpec(memory_space=pl.ANY)
    vmem = pl.BlockSpec(memory_space=pltpu.VMEM)
    dma = pltpu.SemaphoreType.DMA
    message = lambda tiles: pltpu.VMEM((WAVES, tiles, TILE, LANES), BF16)
    flux = pl.pallas_call(
        kernel,
        out_shape=jax.ShapeDtypeStruct((1, ROWS, 8, TOP), BF16),
        in_specs=[anywhere] * 3,
        out_specs=vmem,
        scratch_shapes=[
            pltpu.SMEM((TOP,), jnp.int32),
            pltpu.SMEM((TOP,), jnp.int32),
            pltpu.VMEM((16, LANES), jnp.int32),
            pltpu.VMEM((10, ROWS_PAD, LANES), F32),
            pltpu.VMEM((10, ROWS_PAD, LANES), F32),
            pltpu.VMEM((8 * TAB_STRIDE[0], LANES), F32),
            pltpu.VMEM((8 * TAB_STRIDE[1], LANES), F32),
            pltpu.VMEM((8 * TAB_STRIDE[2], LANES), F32),
            pltpu.VMEM((XPAD, COLS), BF16),
            pltpu.VMEM((XPAD, COLS), BF16),
            pltpu.VMEM((COLS, XPAD), BF16),
            pltpu.VMEM((COLS, XPAD), BF16),
            pltpu.VMEM((COLS, LANES), F32),
            pltpu.VMEM((LEVS, ROWS, 8, TOP), BF16),
            pltpu.VMEM((LANES * ROWS, LANES), F32),
            message(2), message(3), message(3), message(2), message(3), message(3),
            message(2), message(3), message(3), message(2), message(3), message(3),
            pltpu.VMEM((COLS, LANES), F32),
            pltpu.VMEM((COLS, LANES), F32),
            pltpu.VMEM((COLS, 512), BF16),
            pltpu.VMEM((COLS, 512), BF16),
            pltpu.VMEM((XROWS, 512), F32),
            pltpu.VMEM((XROWS, 512), F32),
            pltpu.VMEM((XPAD, 256), BF16),
            pltpu.VMEM((XPAD, 256), BF16),
            pltpu.VMEM((2, 4, ROWS, 8, TOP), BF16),
            pltpu.VMEM((4, ROWS, 8, TOP), BF16),
            pltpu.VMEM((4, ROWS, 8, TOP), BF16),
            pltpu.VMEM((3, ROWS, 8, TOP), BF16),
            dma((2,)),
            pltpu.SemaphoreType.REGULAR((4,)),
            dma,
            dma((4, GROUPS)), dma((4, GROUPS)), dma((4, GROUPS)), dma((4, GROUPS)),
            dma((3,)), dma((3,)), dma((3,)), dma((3,)),
            dma((GROUPS,)), dma((GROUPS,)), dma((4, GROUPS)), dma((4, GROUPS)),
        ],
        compiler_params=pltpu.CompilerParams(
            collective_id=0, has_side_effects=True, vmem_limit_bytes=60 * 2**20
        ),
        name="flux_transform",
    )(wave_order, truncation, spectra)
    return flux.astype(F32)


def solution(mesh):
    return jax.shard_map(
        on_device,
        mesh=mesh,
        in_specs=(P("lev", "wave", None, None), P(), P()),
        out_specs=P("lev", "wave", None, None),
        check_vma=False,
    )
```

```python
import functools
import math

import jax
import jax.numpy as jnp
from jax import lax
from jax.experimental import pallas as pl
from jax.experimental.pallas import tpu as pltpu
from jax.sharding import PartitionSpec as P

MESH = pl.DeviceIdType.MESH
F32 = jnp.float32
BF16 = jnp.bfloat16

TOP = 1280
LON = 2560
ROWS = 20
ROWS_PAD = 24
WAVES = 64
LEVS = 8
LANES = 128
RESCALE = 16
GROUPS = ROWS // 4
WIDTHS = tuple(TOP - 2 * LANES * g for g in range(GROUPS))
TAB_LEN = (1280, 768, 256)
TAB_STRIDE = (1288, 776, 264)
COLS = WAVES * ROWS
HEAVY_COLS = WAVES * 8
XROWS = 672
XPAD = 768
XBLK = 224
TILE = 4
HEAVY = (0, 1)
MID = (2, 3)
LIGHT = (4,)
HALF = WAVES // 2


def iota(shape, dim):
    return lax.broadcasted_iota(jnp.int32, shape, dim)


def first_latitude(lev):
    return 160 * (lev // 2) + 64 * (lev % 2)


def half_angles(lat0):
    lat = iota((8, LANES), 1) + lat0
    return math.pi / TOP * (lat.astype(F32) + 0.5)


def own_orders(wo_ref, base):
    rows = iota((ROWS_PAD, LANES), 0)
    orders = jnp.full((ROWS_PAD, LANES), TOP, jnp.int32)
    for r in range(ROWS):
        orders = jnp.where(rows == r, wo_ref[base + r], orders)
    return orders


def recurrence_start(wo_ref, base, orders, lat0, alpha_ref, both_ref):
    place = iota((16, LANES), 0) * LANES + iota((16, LANES), 1)
    j = jnp.maximum(place, 1).astype(F32)
    terms = jnp.where((place >= 1) & (place < TOP), jnp.log((2.0 * j + 1.0) / (2.0 * j)), 0.0)
    rows = iota((ROWS_PAD, LANES), 0)
    logs = jnp.zeros((ROWS_PAD, LANES), F32)
    for r in range(ROWS):
        part = jnp.where(place <= wo_ref[base + r], terms, 0.0)
        total = jnp.sum(jnp.sum(part, axis=0, keepdims=True), axis=1, keepdims=True)
        logs = jnp.where(rows == r, total, logs)
    order = orders.astype(F32)
    angles = half_angles(lat0)
    cosine = jnp.cos(angles)
    log_sine = jnp.log(jnp.sin(angles))
    for kb in range(TOP // LANES):
        k = iota((ROWS_PAD, LANES), 1) + (kb * LANES + 1)
        kf = k.astype(F32)
        n = order + kf
        alpha = jnp.sqrt((4.0 * n * n - 1.0) / (kf * (n + order)))
        low = n - 1.0
        beta = jnp.sqrt(
            (kf - 1.0) * (kf - 1.0 + 2.0 * order) / jnp.maximum(4.0 * low * low - 1.0, 1.0)
        )
        kept = orders + k < TOP
        alpha_ref[kb] = jnp.where(kept, alpha, 0.0)
        both_ref[kb] = jnp.where(kept, alpha * beta, 0.0)
    state = []
    for g in range(3):
        part = slice(8 * g, 8 * g + 8)
        scale = 0.5 * math.log(0.5) + 0.5 * logs[part] + order[part] * log_sine
        state += [jnp.zeros((8, LANES), F32), jnp.ones((8, LANES), F32), scale]
    return cosine, state


def recurrence_phase(phase, cosine, state, alpha_ref, both_ref, tabs):
    live, start, stop = ((3, 0, 2), (2, 2, 6), (1, 6, 10))[phase]

    def block(kb, flat):
        st = [tuple(flat[3 * g : 3 * g + 3]) for g in range(live)]
        alpha = alpha_ref[kb]
        both = both_ref[kb]
        for i in range(LANES):
            if i % RESCALE == 0:
                factor = [jnp.exp(s[2]) for s in st]
            for g in range(live):
                prev, cur, scale = st[g]
                rows = pl.ds(kb * LANES + i, 8, stride=TAB_STRIDE[g])
                tabs[g][rows, :] = cur * factor[g]
                part = slice(8 * g, 8 * g + 8)
                fresh = (alpha[part, i : i + 1] * cosine) * cur - both[part, i : i + 1] * prev
                st[g] = (cur, fresh, scale)
            if i % RESCALE == RESCALE - 1:
                for g in range(live):
                    prev, cur, scale = st[g]
                    big = jnp.maximum(jnp.maximum(jnp.abs(prev), jnp.abs(cur)), 1e-30)
                    inv = 1.0 / big
                    st[g] = (prev * inv, cur * inv, scale + jnp.log(big))
        return tuple(v for s in st for v in s)

    return list(lax.fori_loop(start, stop, block, tuple(state[: 3 * live])))


def table_rows(tabs, r, width):
    g = r // 8
    return tabs[g][pl.ds((r % 8) * TAB_STRIDE[g], width), :].astype(BF16)


def sin_cos(phase):
    turns = jnp.floor(phase * (1.0 / LON))
    phase = phase - turns * LON
    quarter = jnp.floor(phase * (4.0 / LON) + 0.5)
    t = (phase - quarter * (LON // 4)) * (2.0 * math.pi / LON)
    t2 = t * t
    s = t * (1.0 + t2 * (-1.0 / 6 + t2 * (1.0 / 120 + t2 * (-1.0 / 5040 + t2 * (1.0 / 362880)))))
    c = 1.0 + t2 * (-0.5 + t2 * (1.0 / 24 + t2 * (-1.0 / 720 + t2 * (1.0 / 40320))))
    odd = (quarter == 1.0) | (quarter == 3.0)
    sine = jnp.where(odd, c, s)
    cosine = jnp.where(odd, s, c)
    sine = jnp.where((quarter == 2.0) | (quarter == 3.0), -sine, sine)
    cosine = jnp.where((quarter == 1.0) | (quarter == 2.0), -cosine, cosine)
    return sine, cosine


def flat_row(tile, half):
    if tile < 2:
        return (2 * half + tile) * LANES
    return (4 + 3 * half + tile - 2) * LANES


def column_orders(wo_ref, z, mt_ref):
    lane = iota((8, LANES), 1)

    @pl.loop(0, COLS // LANES)
    def _(jb):
        half = jnp.where(jb < 4, jb // 2, (jb - 4) // 3)
        tile = jnp.where(jb < 4, jb % 2, 2 + (jb - 4) % 3)
        orders = jnp.zeros((8, LANES), jnp.int32)
        for n in range(8):
            plane = lax.rem(z + 4 + 8 * half + n, 16)
            base = plane * (4 * ROWS) + tile * TILE
            for k in range(16):
                value = wo_ref[base + (k // TILE) * ROWS + k % TILE]
                orders = jnp.where(lane == 16 * n + k, value, orders)
        mt_ref[pl.ds(jb, 1), :] = orders[0:1]


def longitude_tables(mt_ref, cos_xj, sin_xj, cos_jx, sin_jx, even_ref):
    @pl.loop(0, COLS // LANES)
    def _(jb):
        cols = pl.ds(pl.multiple_of(jb * LANES, LANES), LANES)
        mj = mt_ref[pl.ds(jb, 1), :]
        mf = mj.astype(F32)
        sb, cb = sin_cos(mf * iota((32, LANES), 0).astype(F32))
        sa, ca = sin_cos(mf * (32 * iota((24, LANES), 0)).astype(F32))
        for xa in range(XPAD // 32):
            rows = pl.ds(32 * xa, 32)
            if xa > 20:
                cos_xj[rows, cols] = jnp.zeros((32, LANES), BF16)
                sin_xj[rows, cols] = jnp.zeros((32, LANES), BF16)
                continue
            sa1, ca1 = sa[xa : xa + 1], ca[xa : xa + 1]
            c = ca1 * cb - sa1 * sb
            s = sa1 * cb + ca1 * sb
            if xa == 20:
                c = jnp.where(iota((32, LANES), 0) == 0, c, 0.0)
                s = jnp.where(iota((32, LANES), 0) == 0, s, 0.0)
            cos_xj[rows, cols] = c.astype(BF16)
            sin_xj[rows, cols] = s.astype(BF16)
        even = jnp.where(lax.rem(mj, 2) == 0, 1.0, 0.0)
        even_ref[cols, :] = jnp.broadcast_to(even, (LANES, LANES)).T
        for xb in range(XPAD // LANES):
            rows = pl.ds(xb * LANES, LANES)
            cos_jx[cols, rows] = cos_xj[rows, cols].T
            sin_jx[cols, rows] = sin_xj[rows, cols].T


def grid_lane(u):
    slot, v = u // 64, u % 64
    flux = jnp.where(slot == 0, v // 16, v // 8)
    s = jnp.where(slot == 0, v // 8 % 2, v // 4 % 2)
    level = jnp.where(slot == 0, v % 8, v % 4)
    return slot, flux, s, level, (slot == 0) | (v < 32)


def pick_fields():
    row, col = iota((256, 512), 0), iota((256, 512), 1)
    slot, level, s, part, field = row // 128, row // 16 % 8, row // 8 % 2, row // 4 % 2, row % 4
    c_part, side = col // 256, col // 128 % 2
    c_slot, flux, c_s, c_level, used = grid_lane(col % 128)
    wanted = jnp.where(side == 0, flux % 2, 2 + flux // 2)
    same = used & (slot == c_slot) & (s == c_s) & (level == c_level)
    same = same & (part == c_part) & (field == wanted)
    return jnp.where(same, 1.0, 0.0).astype(BF16)


def place_fluxes():
    row, col = iota((256, 256), 0), iota((256, 256), 1)
    part = row // 128
    slot, flux, s, level, used = grid_lane(row % 128)
    c_slot = col // 128
    c_level = jnp.where(c_slot == 0, col // 16 % 8, col // 16 % 4)
    same = used & (slot == c_slot) & (level == c_level) & (s == col // 8 % 2)
    same = same & (part == col // 4 % 2) & (flux == col % 4)
    return jnp.where(same, 1.0, 0.0).astype(BF16)


def kernel(
    wo_hbm, trunc_hbm, spec_ref, out_ref,
    wo_ref, trunc_ref, mt_ref,
    alpha_ref, both_ref, tab0, tab1, tab2,
    cos_xj, sin_xj, cos_jx, sin_jx, even_ref,
    gath, stage,
    send_fl, send_fm, send_fh, recv_fl, recv_fm, recv_fh,
    send_bl, send_bm, send_bh, recv_bl, recv_bm, recv_bh,
    flat0, flat1, x_re, x_im, acc_c, acc_s, h_c, h_s,
    partial, e1_recv, e2_send, e2_recv,
    in_sem, ready, own_sem, g_send, g_recv, c_send, c_recv,
    f_ss, f_rs, b_ss, b_rs,
    e1_ss, e1_rs, e2_ss, e2_rs,
):
    me = lax.axis_index("wave")
    lev = lax.axis_index("lev")
    y = lev // 2
    core = lev % 2
    partner = y * 2 + (1 - core)
    x = lax.rem(me, 4)
    z = me // 4
    tabs = (tab0, tab1, tab2)
    lane4 = iota((TILE, LANES), 1)

    inputs = (
        pltpu.make_async_copy(wo_hbm, wo_ref, in_sem.at[0]),
        pltpu.make_async_copy(trunc_hbm, trunc_ref, in_sem.at[1]),
    )
    for copy in inputs:
        copy.start()

    def z_peer(i):
        return lax.rem(me + 4 * i + WAVES, WAVES)

    def x_peer(i):
        return me - x + lax.rem(x + i, 4)

    barrier = pltpu.get_barrier_semaphore()
    for i in range(1, 4):
        pl.semaphore_signal(
            barrier, inc=1, device_id=(me, lax.rem(lev + 2 * i, LEVS)), device_id_type=MESH
        )
    pl.semaphore_signal(barrier, inc=1, device_id=(me, partner), device_id_type=MESH)
    for peer in (z_peer(1), z_peer(-1), x_peer(1), x_peer(2), x_peer(3)):
        pl.semaphore_signal(barrier, inc=1, device_id=(peer, lev), device_id_type=MESH)

    def say(step):
        reach = (1, 2, 4)
        if step < 3:
            peers = (z_peer(reach[step]), z_peer(-reach[step]))
        else:
            peers = (x_peer(1), x_peer(2), x_peer(3))
        for peer in peers:
            pl.semaphore_signal(ready.at[step], inc=1, device_id=(peer, lev), device_id_type=MESH)

    def hear(step):
        pl.semaphore_wait(ready.at[step], 2 if step < 3 else 3)

    for copy in inputs:
        copy.wait()
    lat0 = first_latitude(lev)
    orders = own_orders(wo_ref, me * ROWS)
    cosine, state = recurrence_start(wo_ref, me * ROWS, orders, lat0, alpha_ref, both_ref)
    flat1[...] = jnp.zeros_like(flat1)
    h_c[pl.ds(XROWS, XPAD - XROWS), :] = jnp.zeros((XPAD - XROWS, 256), BF16)
    h_s[pl.ds(XROWS, XPAD - XROWS), :] = jnp.zeros((XPAD - XROWS, 256), BF16)

    state = recurrence_phase(0, cosine, state, alpha_ref, both_ref, tabs)
    pl.semaphore_wait(barrier, 9)
    say(0)

    def piece(ref, level, g):
        return ref.at[level, pl.ds(4 * g, 4), :, pl.ds(0, WIDTHS[g])]

    def own_copy():
        return pltpu.make_async_copy(spec_ref.at[0], gath.at[lev], own_sem)

    def y_copy(i, g):
        return pltpu.make_async_remote_copy(
            piece(spec_ref, 0, g), piece(gath, lev, g), g_send.at[i, g], g_recv.at[i, g],
            device_id=(me, lax.rem(lev + 2 * i, LEVS)), device_id_type=MESH,
        )

    def core_copy(i, g):
        level = lax.rem(lev + LEVS - 2 * i, LEVS)
        src = piece(spec_ref, 0, g) if i == 0 else piece(gath, level, g)
        return pltpu.make_async_remote_copy(
            src, piece(gath, level, g), c_send.at[i, g], c_recv.at[i, g],
            device_id=(me, partner), device_id_type=MESH,
        )

    def pass_on(groups):
        for g in groups:
            for i in range(1, 4):
                y_copy(i, g).wait()
                core_copy(i, g).start()

    def gathered(groups):
        for g in groups:
            for i in range(4):
                core_copy(i, g).wait()

    for groups in (LIGHT, MID, HEAVY):
        for g in groups:
            for i in (2, 1, 3):
                y_copy(i, g).start()
        for g in groups:
            core_copy(0, g).start()
        if groups == LIGHT:
            own_copy().start()
            hear(0)
            say(1)

    angles = half_angles(lat0)[0:1]
    lane = iota((1, LANES), 1)
    cut = jnp.zeros((1, LANES), jnp.int32)
    for n in range(LANES):
        cut = jnp.where(lane == n, trunc_ref[lat0 + n], cut)
    area = (float(TOP) / LON) * (math.pi / TOP) * jnp.sin(angles)
    area = jnp.where(iota((1, LANES), 1) < 64 + 32 * core, area, 0.0)
    sign = jnp.where(iota((1, TOP), 1) % 2 == 0, 1.0, -1.0)

    def legendre_row(r):
        width = WIDTHS[r // 4]
        table = table_rows(tabs, r, width)
        coeff = gath[:, r, :, 0:width].astype(F32)
        both_signs = jnp.stack([coeff, coeff * sign[:, :width]], axis=1).reshape(LANES, width)
        fourier = jnp.dot(both_signs.astype(BF16), table, preferred_element_type=F32)
        order = wo_ref[me * ROWS + r]
        weight = jnp.where(order == 0, 1.0, 2.0)
        fourier = fourier * jnp.where(order < cut, weight, 0.0)
        stage[pl.ds(r // TILE * 512 + r % TILE, LANES, stride=TILE), :] = fourier.T

    def both_cores(tiles, act):
        @pl.when(core == 0)
        def _():
            act(len(tiles))

        @pl.when(core == 1)
        def _():
            act(len(tiles) + 1)

    def peer(half, t):
        return lax.rem(z + 4 + 8 * half + t // 4, 16) * 4 + lax.rem(t, 4)

    def send_half(bufs, half):
        send, recv, ss, rs, tiles = bufs

        def start(count):
            @pl.loop(0, HALF, unroll=4)
            def _(t):
                to = peer(half, t)

                @pl.when(to != me)
                def _():
                    pltpu.make_async_remote_copy(
                        send.at[to, pl.ds(0, count)], recv.at[me, pl.ds(0, count)], ss, rs,
                        device_id=(to, lev), device_id_type=MESH,
                    ).start()

        both_cores(tiles, start)
        if half == 1:
            recv[me] = send[me]

    def wait_all(bufs):
        send, recv, ss, rs, tiles = bufs

        def wait(count):
            window = (pl.ds(0, WAVES - 1), pl.ds(0, count))
            pltpu.make_async_copy(send.at[window], send.at[window], ss).wait()
            pltpu.make_async_copy(recv.at[window], recv.at[window], rs).wait()

        both_cores(tiles, wait)

    fl = (send_fl, recv_fl, f_ss.at[0], f_rs.at[0], LIGHT)
    fm = (send_fm, recv_fm, f_ss.at[1], f_rs.at[1], MID)
    fh = (send_fh, recv_fh, f_ss.at[2], f_rs.at[2], HEAVY)
    bl = (send_bl, recv_bl, b_ss.at[0], b_rs.at[0], LIGHT)
    bm = (send_bm, recv_bm, b_ss.at[1], b_rs.at[1], MID)
    bh = (send_bh, recv_bh, b_ss.at[2], b_rs.at[2], HEAVY)

    def pack(bufs):
        send, tiles = bufs[0], bufs[4]
        one, two = tiles[0], tiles[-1]

        @pl.loop(0, WAVES, unroll=8)
        def _(w):
            for q, tile in enumerate(tiles):
                send[w, q] = stage[pl.ds(tile * 512 + TILE * w, TILE), :].astype(BF16)

        @pl.when(core == 1)
        def _():
            @pl.loop(0, HALF, unroll=8)
            def _(e):
                place = TILE * (WAVES + e)
                q = len(tiles)
                first = stage[pl.ds(one * 512 + place, TILE), :]
                second = pltpu.roll(stage[pl.ds(two * 512 + place, TILE), :], 64, 1)
                send[2 * e, q] = jnp.where(lane4 < 64, first, second).astype(BF16)
                send[2 * e + 1, q] = jnp.where(lane4 < 64, second, first).astype(BF16)

    hear(1)
    say(2)
    state = recurrence_phase(1, cosine, state, alpha_ref, both_ref, tabs)
    hear(2)
    say(3)
    pass_on(LIGHT)
    recurrence_phase(2, cosine, state, alpha_ref, both_ref, tabs)
    own_copy().wait()
    for bufs in (fl, fm, fh):
        groups = bufs[4]
        if groups != LIGHT:
            pass_on(groups)
        gathered(groups)
        for g in groups:
            for r in range(4 * g, 4 * g + 4):
                legendre_row(r)
        pack(bufs)
        if groups == LIGHT:
            hear(3)
        send_half(bufs, 0)
        send_half(bufs, 1)

    column_orders(wo_ref, z, mt_ref)
    longitude_tables(mt_ref, cos_xj, sin_xj, cos_jx, sin_jx, even_ref)

    fields = pick_fields()

    def unpack(bufs):
        recv, tiles = bufs[1], bufs[4]
        one, two = tiles[0], tiles[-1]
        odd = me % 2 == 1
        for half in range(2):

            @pl.loop(0, HALF, unroll=8)
            def _(t):
                for q, tile in enumerate(tiles):
                    place = pl.ds(flat_row(tile, half) + TILE * t, TILE)
                    flat0[place, :] = recv[peer(half, t), q].astype(F32)

            @pl.when(core == 1)
            def _():
                @pl.loop(0, HALF, unroll=8)
                def _(t):
                    here = recv[peer(half, t), len(tiles)].astype(F32)
                    there = pltpu.roll(here, 64, 1)
                    place = pl.ds(flat_row(one, half) + TILE * t, TILE)
                    flat1[place, :] = jnp.where(odd, there, here)
                    if two != one:
                        place = pl.ds(flat_row(two, half) + TILE * t, TILE)
                        flat1[place, :] = jnp.where(odd, here, there)

    def build(first_row, count):
        @pl.loop(0, count // LANES)
        def _(b):
            rows = pl.ds(pl.multiple_of(first_row + b * LANES, LANES), LANES)
            raw = jnp.concatenate([flat0[rows, :], flat1[rows, :]], axis=1).astype(BF16)
            picked = jnp.dot(raw, fields, preferred_element_type=F32)
            even = even_ref[rows, :]
            even = jnp.concatenate([even, even], axis=1)
            for part, ref in ((0, x_re), (1, x_im)):
                both = picked[:, 256 * part : 256 * part + 256]
                evens = both * even
                ref[rows, :] = jnp.concatenate([evens, both - evens], axis=1).astype(BF16)

    heavy = pl.ds(0, HEAVY_COLS)
    light = pl.ds(HEAVY_COLS, COLS - HEAVY_COLS)

    wait_all(fl)
    unpack(fl)
    wait_all(fm)
    unpack(fm)
    build(HEAVY_COLS, COLS - HEAVY_COLS)

    @pl.loop(0, XROWS // XBLK)
    def _(b):
        rows = pl.ds(pl.multiple_of(b * XBLK, 16), XBLK)
        acc_c[rows, :] = jnp.dot(cos_xj[rows, light], x_re[light, :], preferred_element_type=F32)
        acc_s[rows, :] = jnp.dot(sin_xj[rows, light], x_im[light, :], preferred_element_type=F32)

    wait_all(fh)
    unpack(fh)
    build(0, HEAVY_COLS)

    @pl.loop(0, XROWS // XBLK)
    def _(b):
        rows = pl.ds(pl.multiple_of(b * XBLK, 16), XBLK)
        c = acc_c[rows, :] + jnp.dot(
            cos_xj[rows, heavy], x_re[heavy, :], preferred_element_type=F32
        )
        s = acc_s[rows, :] + jnp.dot(
            sin_xj[rows, heavy], x_im[heavy, :], preferred_element_type=F32
        )
        c_sum, c_dif = c[:, :256] + c[:, 256:], c[:, :256] - c[:, 256:]
        s_sum, s_dif = s[:, :256] + s[:, 256:], s[:, :256] - s[:, 256:]

        def flux(g):
            return g[:, :128] * g[:, 128:]

        place = iota((XBLK, LANES), 0) + b * XBLK
        once = jnp.where((place == 0) | (place == LON // 4), 0.5, 1.0)
        f1 = flux(c_sum - s_sum) * once
        f2 = flux(c_sum + s_sum) * once
        f3 = flux(c_dif + s_dif) * once
        f4 = flux(c_dif - s_dif) * once
        near, far = f1 + f2, f3 + f4
        near_d, far_d = f2 - f1, f3 - f4
        h_c[rows, :] = jnp.concatenate([near + far, near - far], axis=1).astype(BF16)
        h_s[rows, :] = jnp.concatenate([near_d + far_d, near_d - far_d], axis=1).astype(BF16)

    places = place_fluxes()

    def direct(first_row, count):
        rows = pl.ds(first_row, count)
        c = jnp.dot(cos_jx[rows, :], h_c[...], preferred_element_type=F32)
        s = jnp.dot(sin_jx[rows, :], h_s[...], preferred_element_type=F32)
        even = even_ref[rows, :] > 0.5
        c = jnp.where(even, c[:, :128], c[:, 128:])
        s = jnp.where(even, s[:, :128], s[:, 128:])
        back = jnp.dot(
            jnp.concatenate([c, s], axis=1).astype(BF16), places, preferred_element_type=F32
        )
        flat0[rows, :] = back[:, :LANES]
        flat1[rows, :] = back[:, LANES:]

    def pack_back(bufs, half):
        send, tiles = bufs[0], bufs[4]
        one, two = tiles[0], tiles[-1]

        @pl.loop(0, HALF, unroll=8)
        def _(t):
            for q, tile in enumerate(tiles):
                place = pl.ds(flat_row(tile, half) + TILE * t, TILE)
                send[peer(half, t), q] = flat0[place, :].astype(BF16)

        @pl.when(core == 1)
        def _():
            @pl.loop(0, HALF, unroll=8)
            def _(t):
                first = flat1[pl.ds(flat_row(one, half) + TILE * t, TILE), :]
                second = flat1[pl.ds(flat_row(two, half) + TILE * t, TILE), :]
                both = jnp.where(lane4 < 64, first, second).astype(BF16)
                send[peer(half, t), len(tiles)] = both

    for half in range(2):
        direct(half * 256, 256)
        pack_back(bh, half)
        send_half(bh, half)
    for half in range(2):
        direct(HEAVY_COLS + half * 384, 384)
        pack_back(bm, half)
        send_half(bm, half)
    for half in range(2):
        pack_back(bl, half)
        send_half(bl, half)

    def unpack_back(bufs):
        recv, tiles = bufs[1], bufs[4]
        one, two = tiles[0], tiles[-1]

        @pl.loop(0, WAVES, unroll=8)
        def _(w):
            for q, tile in enumerate(tiles):
                stage[pl.ds(tile * 512 + TILE * w, TILE), :] = recv[w, q].astype(F32)

        @pl.when(core == 1)
        def _():
            @pl.loop(0, HALF, unroll=8)
            def _(e):
                place = TILE * (WAVES + e)
                low = recv[2 * e, len(tiles)].astype(F32)
                high = recv[2 * e + 1, len(tiles)].astype(F32)
                first = jnp.where(lane4 < 64, low, pltpu.roll(high, 64, 1))
                stage[pl.ds(one * 512 + place, TILE), :] = first
                if two != one:
                    second = jnp.where(lane4 < 64, pltpu.roll(low, 64, 1), high)
                    stage[pl.ds(two * 512 + place, TILE), :] = second

    def e1_copy(g):
        window = (slice(None), pl.ds(4 * g, 4), slice(None), pl.ds(0, WIDTHS[g]))
        return pltpu.make_async_remote_copy(
            partial.at[(1 - core,) + window], e1_recv.at[window], e1_ss.at[g], e1_rs.at[g],
            device_id=(me, partner), device_id_type=MESH,
        )

    def e2_copy(i, g):
        to = lax.rem(y + i, 4)
        return pltpu.make_async_remote_copy(
            piece(e2_send, to, g), piece(e2_recv, i - 1, g), e2_ss.at[i, g], e2_rs.at[i, g],
            device_id=(me, to * 2 + core), device_id_type=MESH,
        )

    def add_cores(g):
        e1_copy(g).wait()
        for r in range(4 * g, 4 * g + 4):
            for q in range(4):
                mine = partial[core, q, r, :, 0 : WIDTHS[g]].astype(F32)
                other = e1_recv[q, r, :, 0 : WIDTHS[g]].astype(F32)
                e2_send[q, r, :, 0 : WIDTHS[g]] = (mine + other).astype(BF16)
        for i in (2, 1, 3):
            e2_copy(i, g).start()

    def flux_rows(g):
        width = WIDTHS[g]
        for r in range(4 * g, 4 * g + 4):
            table = table_rows(tabs, r, width)
            order = wo_ref[me * ROWS + r]
            weight = jnp.where(order == 0, 1.0, 0.5)
            factor = jnp.where(order < cut, area * weight, 0.0)
            back = stage[pl.ds(r // TILE * 512 + r % TILE, LANES, stride=TILE), :]
            sums = lax.dot_general(
                (back.T * factor).astype(BF16), table, (((1,), (1,)), ((), ())),
                preferred_element_type=F32,
            )
            sums = sums.reshape(LEVS, 2, 8, width)
            sums = (sums[:, 0] + sums[:, 1] * sign[:, :width]).astype(BF16)
            for l in range(LEVS):
                partial[l % 2, l // 2, r, :, 0:width] = sums[l]
        e1_copy(g).start()

    def finish(g):
        width = WIDTHS[g]
        for i in range(1, 4):
            e2_copy(i, g).wait()
        for r in range(4 * g, 4 * g + 4):
            total = e2_send[y, r, :, 0:width].astype(F32)
            for i in range(3):
                total = total + e2_recv[i, r, :, 0:width].astype(F32)
            out_ref[0, r, :, 0:width] = total.astype(BF16)
            if width < TOP:
                out_ref[0, r, :, width:TOP] = jnp.zeros((8, TOP - width), BF16)

    for bufs in (bh, bm, bl):
        groups = bufs[4]
        wait_all(bufs)
        unpack_back(bufs)
        for g in groups:
            flux_rows(g)
        for g in groups:
            add_cores(g)
    for g in range(GROUPS):
        finish(g)


def on_device(spectra, wave_order, truncation):
    anywhere = pl.BlockSpec(memory_space=pl.ANY)
    vmem = pl.BlockSpec(memory_space=pltpu.VMEM)
    dma = pltpu.SemaphoreType.DMA
    message = lambda tiles: pltpu.VMEM((WAVES, tiles, TILE, LANES), BF16)
    flux = pl.pallas_call(
        kernel,
        out_shape=jax.ShapeDtypeStruct((1, ROWS, 8, TOP), BF16),
        in_specs=[anywhere] * 3,
        out_specs=vmem,
        scratch_shapes=[
            pltpu.SMEM((TOP,), jnp.int32),
            pltpu.SMEM((TOP,), jnp.int32),
            pltpu.VMEM((16, LANES), jnp.int32),
            pltpu.VMEM((10, ROWS_PAD, LANES), F32),
            pltpu.VMEM((10, ROWS_PAD, LANES), F32),
            pltpu.VMEM((9 * TAB_STRIDE[0], LANES), F32),
            pltpu.VMEM((9 * TAB_STRIDE[1], LANES), F32),
            pltpu.VMEM((9 * TAB_STRIDE[2], LANES), F32),
            pltpu.VMEM((XPAD, COLS), BF16),
            pltpu.VMEM((XPAD, COLS), BF16),
            pltpu.VMEM((COLS, XPAD), BF16),
            pltpu.VMEM((COLS, XPAD), BF16),
            pltpu.VMEM((COLS, LANES), F32),
            pltpu.VMEM((LEVS, ROWS, 8, TOP), BF16),
            pltpu.VMEM((LANES * ROWS + 8, LANES), F32),
            message(2), message(3), message(3), message(2), message(3), message(3),
            message(2), message(3), message(3), message(2), message(3), message(3),
            pltpu.VMEM((COLS, LANES), F32),
            pltpu.VMEM((COLS, LANES), F32),
            pltpu.VMEM((COLS, 512), BF16),
            pltpu.VMEM((COLS, 512), BF16),
            pltpu.VMEM((XROWS, 512), F32),
            pltpu.VMEM((XROWS, 512), F32),
            pltpu.VMEM((XPAD, 256), BF16),
            pltpu.VMEM((XPAD, 256), BF16),
            pltpu.VMEM((2, 4, ROWS, 8, TOP), BF16),
            pltpu.VMEM((4, ROWS, 8, TOP), BF16),
            pltpu.VMEM((4, ROWS, 8, TOP), BF16),
            pltpu.VMEM((3, ROWS, 8, TOP), BF16),
            dma((2,)),
            pltpu.SemaphoreType.REGULAR((4,)),
            dma,
            dma((4, GROUPS)), dma((4, GROUPS)), dma((4, GROUPS)), dma((4, GROUPS)),
            dma((3,)), dma((3,)), dma((3,)), dma((3,)),
            dma((GROUPS,)), dma((GROUPS,)), dma((4, GROUPS)), dma((4, GROUPS)),
        ],
        compiler_params=pltpu.CompilerParams(
            collective_id=0, has_side_effects=True, vmem_limit_bytes=60 * 2**20
        ),
        name="flux_transform",
    )(wave_order, truncation, spectra)
    return flux.astype(F32)


def solution(mesh):
    return jax.shard_map(
        on_device,
        mesh=mesh,
        in_specs=(P("lev", "wave", None, None), P(), P()),
        out_specs=P("lev", "wave", None, None),
        check_vma=False,
    )
```
